32 devices in a mesh: pair: 4 (over x, core), grow: 2 (over y), gcol: 4 (over z).
Axes of the slice: x: 2, y: 2, z: 4, core: 2. Of those that a mesh axis runs over, the one named last changes fastest.
Arguments:
- valence: bfloat16 [48, 32768], replicated, may hold values from -6 to 6
- conduction: bfloat16 [64, 32768], P('pair'), may hold values from -6 to 6
- valence_energy: float32 [48], replicated, may hold values from -12 to -1
- conduction_energy: float32 [64], P('pair'), may hold values from 0.5 to 8
- pair_valence: int32 [64], P(('pair', 'grow', 'gcol')), may hold values from 0 to 47
- pair_conduction: int32 [64], P(('pair', 'grow', 'gcol')), may hold values from 0 to 15
- pair_count: int32 [32], P(('pair', 'grow', 'gcol')), may hold values from 1 to 2, as said below
- g_index: int32 [9216], replicated, may hold values from 1 to 32767, as said below
Outputs:
- chi: float32 [9216, 9216], P(('pair', 'grow'), 'gcol')
The draws below stay inside these ranges and needn't reach their ends.
Inputs may be any that keep to these rules, and one draw needn't show every extreme that they name: `pair_count`: every device has at least one live slot, and some device has exactly 2. `g_index`: distinct cells; with centred frequencies (an index v stands for v - 32 when v >= 16) they are the 9216 cells of smallest |G| other than G = 0 and the planes at frequency -16, closed under G -> -G, in no particular order.
All inputs are finite; a program needn't handle non-finite values.
Results may differ from the reference program's by a relative error of at most 0.0037.
Values may be sent and summed in bfloat16 or wider, within the bound.
A program may use at most 128 MiB of HBM per device.

```python
import jax
import jax.numpy as jnp
from jax import lax

NV = 48
GRID = 32
NG = 9216
CB_DEV = 16
P_MAX = 2
CB = 64
SLOTS = 64
GRID3 = 32768
N_GROW = 2
N_GCOL = 4


def draw_pair_count(key, part):
    key = jax.random.fold_in(key, 11)
    first, second = jax.random.split(key)
    devices_total = SLOTS // P_MAX
    counts = jax.random.randint(first, (devices_total,), 1, P_MAX + 1)
    position = jax.random.randint(second, (), 0, devices_total)
    return counts.at[position].set(P_MAX).astype(jnp.int32)


def centred(values):
    return jnp.where(values < GRID // 2, values, values - GRID)


def draw_g_index(key, part):
    key = jax.random.fold_in(key, 23)
    first, second = jax.random.split(key)
    cells = jnp.arange(GRID3, dtype=jnp.int32)
    first_idx = cells // (GRID * GRID)
    second_idx = cells // GRID % GRID
    third_idx = cells % GRID
    partner = ((GRID - first_idx) % GRID * GRID + (GRID - second_idx) % GRID) * GRID + (GRID - third_idx) % GRID
    canonical = jnp.minimum(cells, partner)
    ties = jax.random.permutation(first, GRID3).astype(jnp.int32)[canonical]
    radius = centred(first_idx) ** 2 + centred(second_idx) ** 2 + centred(third_idx) ** 2
    excluded = (first_idx == GRID // 2) | (second_idx == GRID // 2) | (third_idx == GRID // 2) | (cells == 0)
    radius = jnp.where(excluded, 3 * GRID * GRID, radius)
    score = (radius * GRID3 + ties) * 2 + (cells > partner).astype(jnp.int32)
    chosen = jnp.argsort(score, stable=True)[:NG].astype(jnp.int32)
    return jax.random.permutation(second, chosen).astype(jnp.int32)


def place_ends(result, rng, low, largest):
    index_at = [jax.random.randint(jax.random.fold_in(rng, axis), (), 0, length) for axis, length in enumerate(result.shape)]
    main_axis = result.shape.index(max(result.shape))
    next_to = index_at[:main_axis] + [(index_at[main_axis] + 1) % result.shape[main_axis]] + index_at[main_axis + 1:]
    return result.at[tuple(index_at)].set(low).at[tuple(next_to)].set(largest)


def shard_levels(key, shape, cuts, low, high):
    level, own = 1.0, jax.random.fold_in(key, 6)
    for axis_at, shards_of in cuts:
        draws = jnp.exp(jax.random.uniform(jax.random.fold_in(own, axis_at), (shards_of,), jnp.float32, low / len(cuts), high / len(cuts)))
        level = level * jnp.repeat(draws, shape[axis_at] // shards_of).reshape([-1 if axis == axis_at else 1 for axis in range(len(shape))])
    return level


def gaussian(stream_key, extent, width, limit, cuts=(), kind=jnp.bfloat16):
    result = jax.random.normal(stream_key, extent, jnp.float32) * width
    if len(cuts) > 0:
        result = shard_levels(stream_key, extent, cuts, -0.22, 0.18) * result
    return jnp.clip(result, min=-limit, max=limit).astype(kind)


def setup_inputs(seed: int = 0) -> dict:
    key_list = jax.random.split(jax.random.key(seed), 9)
    return {
        "valence": gaussian(key_list[0], (NV, GRID3), 1.0, 6.0),
        "conduction": gaussian(key_list[1], (CB, GRID3), 1.0, 6.0, ((0, 4),)),
        "valence_energy": jnp.clip(jax.random.uniform(key_list[2], (NV,), jnp.float32, -12.0, -1.0), -12.0, -1.0),
        "conduction_energy": jnp.clip(0.5 + 7.5 * jax.random.uniform(key_list[3], (CB,), jnp.float32) ** shard_levels(key_list[3], (CB,), ((0, 4),), -0.2, 0.2), 0.5, 8.0),
        "pair_valence": place_ends(jax.random.randint(key_list[4], (SLOTS,), 0, NV), jax.random.fold_in(key_list[4], 1), 0, NV - 1).astype(jnp.int32),
        "pair_conduction": place_ends(jax.random.randint(key_list[5], (SLOTS,), 0, CB_DEV), jax.random.fold_in(key_list[5], 1), 0, CB_DEV - 1).astype(jnp.int32),
        "pair_count": draw_pair_count(jax.random.fold_in(key_list[8], 71), 0),
        "g_index": draw_g_index(jax.random.fold_in(key_list[8], 71), 0),
    }


def reference(valence, conduction, valence_energy, conduction_energy, pair_valence, pair_conduction, pair_count, g_index):
    slot_ids = jnp.arange(SLOTS, dtype=jnp.int32)
    device_ids = slot_ids // P_MAX
    group_ids = device_ids // (N_GROW * N_GCOL)
    cband = (group_ids * CB_DEV + pair_conduction).astype(jnp.int32)
    live_slots = (slot_ids % P_MAX < pair_count[device_ids]).astype(jnp.float32)
    energy_gap = conduction_energy[cband] - valence_energy[pair_valence]
    factor = live_slots * jnp.sqrt(4.0 / energy_gap) / jnp.sqrt(jnp.float32(GRID3))

    def one_device(inputs):
        vband, cidx, scale = inputs
        density = valence[vband].astype(jnp.float32) * conduction[cidx].astype(jnp.float32)
        spectrum = jnp.fft.fftn(density.reshape(-1, GRID, GRID, GRID), axes=(1, 2, 3)).reshape(-1, GRID3)
        chosen = spectrum[:, g_index]
        real_part = (jnp.real(chosen) * scale[:, None]).astype(jnp.bfloat16)
        imag_part = (jnp.imag(chosen) * scale[:, None]).astype(jnp.bfloat16)
        return (real_part, imag_part)
    blocks = SLOTS // P_MAX
    real_rows, imag_rows = lax.map(one_device, (pair_valence.reshape(blocks, P_MAX), cband.reshape(blocks, P_MAX), factor.reshape(blocks, P_MAX)))
    amplitude = jnp.concatenate([real_rows.reshape(SLOTS, NG), imag_rows.reshape(SLOTS, NG)], axis=0).astype(jnp.float32)
    product = jnp.dot(amplitude.T, amplitude, preferred_element_type=jnp.float32, precision=lax.Precision.HIGHEST)
    return -product / jnp.sqrt(jnp.float32(SLOTS))
```

```python
import functools
import math

import jax
import jax.numpy as jnp
import ml_dtypes
import numpy as np
from jax import lax
from jax.experimental import pallas as pl
from jax.experimental.pallas import tpu as pltpu
from jax.sharding import PartitionSpec as P

GRID = 32
CHUNK = 16
LANES = 128
TILE = 256
MAIN = 256
MESH = pl.DeviceIdType.MESH
BF16 = jnp.bfloat16
F32 = jnp.float32


def pad_to(size, unit):
    return -(-size // unit) * unit


def ball(total_g):
    freq = np.arange(-(GRID // 2) + 1, GRID // 2)
    square = freq[:, None, None] ** 2 + freq[None, :, None] ** 2 + freq[None, None, :] ** 2
    return int(np.sort(square.ravel())[total_g])


def split(values):
    high = values.astype(ml_dtypes.bfloat16)
    low = (values - high.astype(np.float64)).astype(ml_dtypes.bfloat16)
    return high, low


def tables(total_g):
    limit = ball(total_g)
    reach = math.isqrt(limit)
    plane = []
    for b in range(0, reach + 1):
        for c in range(-reach, reach + 1):
            if b * b + c * c <= limit and (b > 0 or c >= 0):
                plane.append((b * b + c * c, b, c))
    plane.sort()
    extra = plane[MAIN:]
    short = math.isqrt(limit - extra[0][0]) if extra else -1
    width = pad_to(len(plane), LANES)
    keys = np.full((width,), -1, np.int32)
    bs = np.zeros((width,), np.int64)
    cs = np.zeros((width,), np.int64)
    for at, (_, b, c) in enumerate(plane):
        keys[at] = b * GRID + c + GRID // 2
        bs[at], cs[at] = b, c
    cell = np.arange(GRID * GRID)
    phase = (cell[:, None] // GRID * bs[None] + cell[:, None] % GRID * cs[None]) % GRID
    angle = phase * (2.0 * math.pi / GRID)
    used = keys[None] >= 0
    first = np.concatenate([np.cos(angle) * used, -np.sin(angle) * used], axis=1)
    a = np.arange(-reach, reach + 1)
    angle = (a[:, None] * np.arange(GRID)[None] % GRID) * (2.0 * math.pi / GRID)
    small = np.zeros((len(a), 2, 2, GRID))
    small[:, 0, 0], small[:, 0, 1] = np.cos(angle), np.sin(angle)
    small[:, 1, 0], small[:, 1, 1] = -np.sin(angle), np.cos(angle)
    small = small.reshape(len(a) * 2, 2 * GRID)
    second = np.kron(small, np.eye(CHUNK))
    keys = np.repeat(keys[:, None], TILE, axis=1)
    return reach, short, width, keys, split(first), split(second)


def amplitude_kernel(
    reach, short, width, tiles,
    info, energy_v, energy_c, g_list, valence, conduction, keys,
    first_h, first_l, second_h, second_l,
    out, dens_h, dens_l, next_h, next_l, spec,
):
    n_v, n_c = valence.shape[0], conduction.shape[0]
    plane = GRID * GRID
    pick_v = info[:, 0:1] == lax.broadcasted_iota(jnp.int32, (CHUNK, n_v), 1)
    pick_c = info[:, 1:2] == lax.broadcasted_iota(jnp.int32, (CHUNK, n_c), 1)
    live = info[:, 2:3].astype(F32)
    gap = jnp.sum(jnp.where(pick_c, energy_c[...], 0.0), axis=1, keepdims=True) - jnp.sum(
        jnp.where(pick_v, energy_v[...], 0.0), axis=1, keepdims=True
    )
    factor = live * jnp.sqrt(4.0 / gap) / math.sqrt(GRID**3)
    one_v = jnp.where(pick_v, 1.0, 0.0).astype(BF16)
    one_c = jnp.where(pick_c, 1.0, 0.0).astype(BF16)
    dot = functools.partial(jnp.dot, preferred_element_type=F32)

    for i in range(GRID):
        at = slice(i * plane, (i + 1) * plane)
        dens = dot(one_v, valence[:, at]) * dot(one_c, conduction[:, at])
        high = dens.astype(BF16)
        rows = slice(i * CHUNK, (i + 1) * CHUNK)
        dens_h[rows, :] = high
        dens_l[rows, :] = (dens - high.astype(F32)).astype(BF16)

    half = GRID * CHUNK
    for part in range(2):
        at = slice(part * width, (part + 1) * width)
        value = (
            dot(dens_h[...], first_h[:, at])
            + dot(dens_l[...], first_h[:, at])
            + dot(dens_h[...], first_l[:, at])
        )
        high = value.astype(BF16)
        next_h[part * half:(part + 1) * half, :] = high
        next_l[part * half:(part + 1) * half, :] = (value - high.astype(F32)).astype(BF16)

    value = (
        dot(second_h[...], next_h[...])
        + dot(second_h[...], next_l[...])
        + dot(second_l[...], next_h[...])
    )
    count = 2 * (2 * reach + 1)
    value = value.reshape(count, CHUNK, width) * factor[None]
    spec[...] = value.reshape(count * CHUNK, width).astype(BF16)

    rows = 2 * CHUNK
    low, high = (reach - short) * rows, (reach + short + 1) * rows

    def tile(t, carry):
        at = pl.ds(pl.multiple_of(t * TILE, TILE), TILE)
        cell = g_list[:, at]
        centre = lambda v: jnp.where(v < GRID // 2, v, v - GRID)
        a = centre(cell // (GRID * GRID))
        b = centre(cell // GRID % GRID)
        c = centre(cell % GRID)
        flip = (b < 0) | ((b == 0) & (c < 0))
        a = jnp.where(flip, -a, a)
        b = jnp.where(flip, -b, b)
        c = jnp.where(flip, -c, c)
        key = b * GRID + c + GRID // 2
        hot = jnp.where(keys[...] == key, 1.0, 0.0).astype(BF16)
        picked = dot(spec[:, :MAIN], hot[:MAIN])
        if width > MAIN:
            more = dot(spec[low:high, MAIN:], hot[MAIN:])
        total = jnp.zeros((rows, TILE), F32)
        for n in range(2 * reach + 1):
            value = picked[n * rows:(n + 1) * rows]
            if width > MAIN and low <= n * rows < high:
                value = value + more[n * rows - low:(n + 1) * rows - low]
            total = jnp.where(a == n - reach, value, total)
        imag = total[CHUNK:]
        out[:CHUNK, at] = total[:CHUNK].astype(BF16)
        out[CHUNK:, at] = jnp.where(flip, -imag, imag).astype(BF16)
        return carry

    lax.fori_loop(0, tiles, tile, 0)


def amplitudes(info, energy_v, energy_c, g_list, valence, conduction, total_g):
    reach, short, width, keys, first, second = tables(total_g)
    length = g_list.shape[1]
    chunks = info.shape[0] // CHUNK
    consts = [jnp.asarray(x) for x in (keys, *first, *second)]
    whole = lambda x: pl.BlockSpec(x.shape, lambda n: (0, 0), pipeline_mode=pl.Buffered(1))
    args = [energy_v, energy_c, g_list, valence, conduction, *consts]
    rows = 2 * CHUNK * (2 * reach + 1)
    half = GRID * CHUNK
    return pl.pallas_call(
        functools.partial(amplitude_kernel, reach, short, width, length // TILE),
        grid=(chunks,),
        out_shape=jax.ShapeDtypeStruct((chunks * 2 * CHUNK, length), BF16),
        in_specs=[pl.BlockSpec((CHUNK, info.shape[1]), lambda n: (n, 0))] + [whole(x) for x in args],
        out_specs=pl.BlockSpec((2 * CHUNK, length), lambda n: (n, 0)),
        scratch_shapes=[
            pltpu.VMEM((half, GRID * GRID), BF16),
            pltpu.VMEM((half, GRID * GRID), BF16),
            pltpu.VMEM((2 * half, width), BF16),
            pltpu.VMEM((2 * half, width), BF16),
            pltpu.VMEM((rows, width), BF16),
        ],
        compiler_params=pltpu.CompilerParams(vmem_limit_bytes=56 * 2**20),
    )(info, *args)


def exchange_kernel(n_pair, col_pad, row_pad, amp, cols, rows, send_sem, recv_sem, own_sem):
    me = lax.axis_index("pair")
    barrier = pltpu.get_barrier_semaphore()
    for step in range(1, n_pair):
        other = lax.rem(me + step, n_pair)
        pl.semaphore_signal(barrier, inc=1, device_id={"pair": other}, device_id_type=MESH)
    pl.semaphore_wait(barrier, n_pair - 1)
    copies = []
    for step in range(1, n_pair):
        other = lax.rem(me + step, n_pair)
        block = pl.ds(pl.multiple_of(col_pad + other * row_pad, LANES), row_pad)
        for which, (source, target) in enumerate(
            ((amp.at[:, pl.ds(0, col_pad)], cols), (amp.at[:, block], rows))
        ):
            copy = pltpu.make_async_remote_copy(
                src_ref=source,
                dst_ref=target.at[me],
                send_sem=send_sem.at[which, step],
                recv_sem=recv_sem.at[which, step],
                device_id={"pair": other},
                device_id_type=MESH,
            )
            copy.start()
            copies.append(copy)
    block = pl.ds(pl.multiple_of(col_pad + me * row_pad, LANES), row_pad)
    own = [
        pltpu.make_async_copy(amp.at[:, pl.ds(0, col_pad)], cols.at[me], own_sem.at[0]),
        pltpu.make_async_copy(amp.at[:, block], rows.at[me], own_sem.at[1]),
    ]
    for copy in own:
        copy.start()
    for copy in own + copies:
        copy.wait()


def exchange(amp, n_pair, col_pad, row_pad):
    height = amp.shape[0]
    return pl.pallas_call(
        functools.partial(exchange_kernel, n_pair, col_pad, row_pad),
        out_shape=[
            jax.ShapeDtypeStruct((n_pair, height, col_pad), BF16),
            jax.ShapeDtypeStruct((n_pair, height, row_pad), BF16),
        ],
        in_specs=[pl.BlockSpec(memory_space=pl.ANY)],
        out_specs=[pl.BlockSpec(memory_space=pl.ANY)] * 2,
        scratch_shapes=[
            pltpu.SemaphoreType.DMA((2, n_pair)),
            pltpu.SemaphoreType.DMA((2, n_pair)),
            pltpu.SemaphoreType.DMA((2,)),
        ],
        compiler_params=pltpu.CompilerParams(collective_id=0, has_side_effects=True),
    )(amp)


def product_kernel(scale, rows, cols, out):
    value = lax.dot_general(
        rows[...], cols[...], (((0,), (0,)), ((), ())), preferred_element_type=F32
    )
    out[...] = value[: out.shape[0], : out.shape[1]] * scale


def product(rows, cols, n_rows, n_cols, scale):
    depth, row_pad = rows.shape
    block = LANES if n_rows % LANES == 0 else n_rows
    return pl.pallas_call(
        functools.partial(product_kernel, scale),
        grid=(n_rows // block,),
        out_shape=jax.ShapeDtypeStruct((n_rows, n_cols), F32),
        in_specs=[
            pl.BlockSpec((depth, pad_to(block, LANES)), lambda n: (0, n)),
            pl.BlockSpec(cols.shape, lambda n: (0, 0)),
        ],
        out_specs=pl.BlockSpec((block, n_cols), lambda n: (n, 0)),
        compiler_params=pltpu.CompilerParams(vmem_limit_bytes=48 * 2**20),
    )(rows, cols)


def local(
    valence,
    conduction,
    valence_energy,
    conduction_energy,
    pair_valence,
    pair_conduction,
    pair_count,
    g_index,
):
    slot_count = pair_valence.shape[0]
    total_g = g_index.shape[0]
    n_pair = lax.axis_size("pair")
    n_grow = lax.axis_size("grow")
    n_gcol = lax.axis_size("gcol")
    live = (jnp.arange(slot_count, dtype=jnp.int32) < pair_count[0]).astype(jnp.int32)
    info = jnp.stack([pair_valence, pair_conduction, live], axis=1)
    info = lax.all_gather(info, ("grow", "gcol"), axis=0, tiled=True)
    sub_rows = total_g // (n_pair * n_grow)
    col_width = total_g // n_gcol
    row_pad, col_pad = pad_to(sub_rows, LANES), pad_to(col_width, LANES)
    col_list = lax.dynamic_slice(g_index, (lax.axis_index("gcol") * col_width,), (col_width,))
    row_list = lax.dynamic_index_in_dim(
        g_index.reshape(n_pair, n_grow, sub_rows), lax.axis_index("grow"), 1, keepdims=False
    )
    row_list = jnp.pad(row_list, ((0, 0), (0, row_pad - sub_rows))).reshape(-1)
    g_list = jnp.concatenate([jnp.pad(col_list, (0, col_pad - col_width)), row_list])
    length = g_list.shape[0]
    g_list = jnp.pad(g_list, (0, pad_to(length, TILE) - length))[None, :]
    amp = amplitudes(
        info, valence_energy[None, :], conduction_energy[None, :], g_list, valence, conduction, total_g
    )
    cols, rows = exchange(amp, n_pair, col_pad, row_pad)
    total_slots = slot_count * n_pair * n_grow * n_gcol
    return product(
        rows.reshape(-1, row_pad), cols.reshape(-1, col_pad), sub_rows, col_width,
        -1.0 / math.sqrt(total_slots),
    )


def solution(mesh):
    return jax.shard_map(
        local,
        mesh=mesh,
        in_specs=(
            P(),
            P("pair", None),
            P(),
            P("pair"),
            P(("pair", "grow", "gcol")),
            P(("pair", "grow", "gcol")),
            P(("pair", "grow", "gcol")),
            P(),
        ),
        out_specs=P(("pair", "grow"), "gcol"),
        check_vma=False,
    )
```

```python
import functools
import math

import jax
import jax.numpy as jnp
import ml_dtypes
import numpy as np
from jax import lax
from jax.experimental import pallas as pl
from jax.experimental.pallas import tpu as pltpu
from jax.sharding import PartitionSpec as P

GRID = 32
CHUNK = 16
LANES = 128
TILE = 256
MAIN = 256
MESH = pl.DeviceIdType.MESH
BF16 = jnp.bfloat16
F32 = jnp.float32


def pad_to(size, unit):
    return -(-size // unit) * unit


def ball(total_g):
    freq = np.arange(-(GRID // 2) + 1, GRID // 2)
    square = freq[:, None, None] ** 2 + freq[None, :, None] ** 2 + freq[None, None, :] ** 2
    return int(np.sort(square.ravel())[total_g])


def split(values):
    high = values.astype(ml_dtypes.bfloat16)
    low = (values - high.astype(np.float64)).astype(ml_dtypes.bfloat16)
    return high, low


def tables(total_g):
    limit = ball(total_g)
    reach = math.isqrt(limit)
    plane = []
    for b in range(0, reach + 1):
        for c in range(-reach, reach + 1):
            if b * b + c * c <= limit and (b > 0 or c >= 0):
                plane.append((b * b + c * c, b, c))
    plane.sort()
    extra = plane[MAIN:]
    short = math.isqrt(limit - extra[0][0]) if extra else -1
    width = pad_to(len(plane), LANES)
    keys = np.full((width,), -1, np.int32)
    bs = np.zeros((width,), np.int64)
    cs = np.zeros((width,), np.int64)
    for at, (_, b, c) in enumerate(plane):
        keys[at] = b * GRID + c + GRID // 2
        bs[at], cs[at] = b, c
    cell = np.arange(GRID * GRID)
    phase = (cell[:, None] // GRID * bs[None] + cell[:, None] % GRID * cs[None]) % GRID
    angle = phase * (2.0 * math.pi / GRID)
    used = keys[None] >= 0
    first = np.concatenate([np.cos(angle) * used, -np.sin(angle) * used], axis=1)
    a = np.arange(-reach, reach + 1)
    angle = (a[:, None] * np.arange(GRID)[None] % GRID) * (2.0 * math.pi / GRID)
    small = np.zeros((len(a), 2, 2, GRID))
    small[:, 0, 0], small[:, 0, 1] = np.cos(angle), np.sin(angle)
    small[:, 1, 0], small[:, 1, 1] = -np.sin(angle), np.cos(angle)
    small = small.reshape(len(a) * 2, 2 * GRID)
    second = np.kron(small, np.eye(CHUNK))
    keys = np.repeat(keys[:, None], TILE, axis=1)
    return reach, short, width, keys, split(first), split(second)


def body(
    reach, short, width, layout,
    tile_info, energy_v, energy_c, g_list, keys, valence_in, conduction_in, *refs,
):
    n_pair, n_grow, n_gcol, per_device, chunks, col_at, row_at = layout
    tables_in, (cols, rows), scratch = refs[:4], refs[4:6], refs[6:]
    valence, conduction, first_h, first_l, second_h, second_l = scratch[:6]
    infos, dens_h, dens_l, next_h, next_l, spec, row_buf = scratch[6:13]
    load_sem, info_send, info_recv, col_send, col_recv, relay_send, relay_recv, row_send, row_recv = scratch[13:]

    me, grow, gcol = lax.axis_index("pair"), lax.axis_index("grow"), lax.axis_index("gcol")
    chip, core = me // 2, me % 2
    n_chip, n_group = n_pair // 2, n_grow * n_gcol
    group = grow * n_gcol + gcol
    sibling = {"pair": chip * 2 + (1 - core)}

    def group_id(step):
        other = (group + step) % n_group
        return {"grow": other // n_gcol, "gcol": other % n_gcol}

    def pair_at(step):
        return (chip + 1 + step // 2) % n_chip * 2 + (core + step % 2) % 2

    own_step = (n_chip - 1) * 2

    loads = [
        pltpu.make_async_copy(source, target, load_sem.at[n])
        for n, (source, target) in enumerate(
            zip((valence_in, conduction_in, *tables_in), scratch[:6])
        )
    ]
    for load in loads:
        load.start()

    barrier = pltpu.get_barrier_semaphore()

    def greet_group(step, carry):
        pl.semaphore_signal(barrier, inc=1, device_id=group_id(step), device_id_type=MESH)
        return carry

    def greet_pair(step, carry):
        @pl.when(step != own_step)
        def _():
            pl.semaphore_signal(
                barrier, inc=1, device_id={"pair": pair_at(step)}, device_id_type=MESH
            )
        return carry

    lax.fori_loop(1, n_group, greet_group, 0)
    lax.fori_loop(0, n_pair, greet_pair, 0)
    pl.semaphore_wait(barrier, n_group - 1 + n_pair - 1)

    def info_copy(step):
        return pltpu.make_async_remote_copy(
            src_ref=tile_info, dst_ref=infos.at[group],
            send_sem=info_send.at[step], recv_sem=info_recv.at[step],
            device_id=group_id(step), device_id_type=MESH,
        )

    def start_info(step, carry):
        info_copy(step).start()
        return carry

    def wait_info(step, carry):
        info_copy(step).wait()
        return carry

    lax.fori_loop(1, n_group, start_info, 0)
    infos[group] = tile_info[...]
    lax.fori_loop(1, n_group, wait_info, 0)

    n_v, n_c = valence.shape[0], conduction.shape[0]
    plane = GRID * GRID
    count = 2 * (2 * reach + 1)
    half = GRID * CHUNK
    together = CHUNK // per_device
    dot = functools.partial(jnp.dot, preferred_element_type=F32)
    loads[0].wait()
    loads[1].wait()

    def transform(n, first_chunk):
        slot = lax.broadcasted_iota(jnp.int32, (CHUNK, LANES), 0)
        info = jnp.zeros((CHUNK, LANES), jnp.int32)
        for d in range(together):
            info = jnp.where(slot // per_device == d, infos[n * together + d], info)
        pick_v = info[:, 0:1] == lax.broadcasted_iota(jnp.int32, (CHUNK, n_v), 1)
        pick_c = info[:, 1:2] == lax.broadcasted_iota(jnp.int32, (CHUNK, n_c), 1)
        live = info[:, 2:3].astype(F32)
        gap = jnp.sum(jnp.where(pick_c, energy_c[...], 0.0), axis=1, keepdims=True) - jnp.sum(
            jnp.where(pick_v, energy_v[...], 0.0), axis=1, keepdims=True
        )
        factor = live * jnp.sqrt(4.0 / gap) / math.sqrt(GRID**3)
        one_v = jnp.where(pick_v, 1.0, 0.0).astype(BF16)
        one_c = jnp.where(pick_c, 1.0, 0.0).astype(BF16)
        for i in range(GRID):
            at = slice(i * plane, (i + 1) * plane)
            dens = dot(one_v, valence[:, at]) * dot(one_c, conduction[:, at])
            high = dens.astype(BF16)
            span = slice(i * CHUNK, (i + 1) * CHUNK)
            dens_h[span, :] = high
            dens_l[span, :] = (dens - high.astype(F32)).astype(BF16)
        if first_chunk:
            loads[2].wait()
            loads[3].wait()
        for part in range(2):
            at = slice(part * width, (part + 1) * width)
            value = (
                dot(dens_h[...], first_h[:, at])
                + dot(dens_l[...], first_h[:, at])
                + dot(dens_h[...], first_l[:, at])
            )
            high = value.astype(BF16)
            next_h[part * half:(part + 1) * half, :] = high
            next_l[part * half:(part + 1) * half, :] = (value - high.astype(F32)).astype(BF16)
        if first_chunk:
            loads[4].wait()
            loads[5].wait()
        value = (
            dot(second_h[...], next_h[...])
            + dot(second_h[...], next_l[...])
            + dot(second_l[...], next_h[...])
        )
        value = value.reshape(count, CHUNK, width) * factor[None]
        spec[n] = value.reshape(count * CHUNK, width).astype(BF16)

    transform(0, True)
    if chunks > 1:
        @pl.loop(1, chunks)
        def _(n):
            transform(n, False)

    height = 2 * CHUNK
    low, high = (reach - short) * height, (reach + short + 1) * height

    def select(n, source, size, out, target):
        cell = g_list[:, pl.ds(pl.multiple_of(source, LANES), size)]
        centre = lambda v: jnp.where(v < GRID // 2, v, v - GRID)
        a = centre(cell // (GRID * GRID))
        b = centre(cell // GRID % GRID)
        c = centre(cell % GRID)
        flip = (b < 0) | ((b == 0) & (c < 0))
        a = jnp.where(flip, -a, a)
        b = jnp.where(flip, -b, b)
        c = jnp.where(flip, -c, c)
        key = b * GRID + c + GRID // 2
        hot = jnp.where(keys[:, :size] == key, 1.0, 0.0).astype(BF16)
        picked = dot(spec[n, :, :MAIN], hot[:MAIN])
        if width > MAIN:
            more = dot(spec[n, low:high, MAIN:], hot[MAIN:])
        total = jnp.zeros((height, size), F32)
        for k in range(2 * reach + 1):
            value = picked[k * height:(k + 1) * height]
            if width > MAIN and low <= k * height < high:
                value = value + more[k * height - low:(k + 1) * height - low]
            total = jnp.where(a == k - reach, value, total)
        imag = total[CHUNK:]
        at = pl.ds(target, size)
        out[n, :CHUNK, at] = total[:CHUNK].astype(BF16)
        out[n, CHUNK:, at] = jnp.where(flip, -imag, imag).astype(BF16)

    def block(source, size, out):
        for n in range(chunks) if chunks == 1 else [None]:
            def run(n):
                @pl.loop(0, size // TILE)
                def _(t):
                    select(n, source + t * TILE, TILE, out, pl.multiple_of(t * TILE, TILE))
                if size % TILE:
                    done = size // TILE * TILE
                    select(n, source + done, size - done, out, done)
            if n is None:
                pl.loop(0, chunks)(run)
            else:
                run(n)

    def col_copy(step):
        peer = (chip + step) % n_chip * 2 + core
        return pltpu.make_async_remote_copy(
            src_ref=cols.at[me], dst_ref=cols.at[me],
            send_sem=col_send.at[step], recv_sem=col_recv.at[step],
            device_id=sibling if step == 0 else {"pair": peer}, device_id_type=MESH,
        )

    def relay_copy(step):
        source = (chip + n_chip - step) % n_chip * 2 + core
        return pltpu.make_async_remote_copy(
            src_ref=cols.at[source], dst_ref=cols.at[source],
            send_sem=relay_send.at[step], recv_sem=relay_recv.at[step],
            device_id=sibling, device_id_type=MESH,
        )

    def row_copy(step):
        return pltpu.make_async_remote_copy(
            src_ref=row_buf.at[step], dst_ref=rows.at[me],
            send_sem=row_send.at[step], recv_sem=row_recv.at[step],
            device_id={"pair": pair_at(step)}, device_id_type=MESH,
        )

    block(col_at(gcol), cols.shape[-1], cols.at[me])
    for step in (*range(1, n_chip), 0):
        col_copy(step).start()

    def row_step(step, carry):
        block(row_at(pair_at(step), grow), rows.shape[-1], row_buf.at[step])

        @pl.when(step != own_step)
        def _():
            row_copy(step).start()
        return carry

    lax.fori_loop(0, own_step, row_step, 0)
    for step in range(1, n_chip):
        col_copy(step).wait_recv()
        relay_copy(step).start()
    lax.fori_loop(own_step, n_pair, row_step, 0)
    rows[me] = row_buf[own_step]

    for step in range(1, n_chip):
        col_copy(step).wait_send()
        relay_copy(step).wait()
    col_copy(0).wait()

    def row_wait(step, carry):
        @pl.when(step != own_step)
        def _():
            row_copy(step).wait()
        return carry

    lax.fori_loop(0, n_pair, row_wait, 0)


def panels(tile_info, energy_v, energy_c, g_list, valence, conduction, total_g, col_pad, row_pad, layout):
    reach, short, width, keys, first, second = tables(total_g)
    n_pair, n_grow, n_gcol, per_device, chunks = layout[:5]
    consts = [jnp.asarray(x) for x in (*first, *second)]
    large = [valence, conduction, *consts]
    args = [tile_info, energy_v, energy_c, g_list, jnp.asarray(keys)]
    height = 2 * CHUNK * (2 * reach + 1)
    half = GRID * CHUNK
    n_group = n_grow * n_gcol
    vmem = pl.BlockSpec(memory_space=pltpu.VMEM)
    dma = pltpu.SemaphoreType.DMA
    return pl.pallas_call(
        functools.partial(body, reach, short, width, layout),
        out_shape=[
            jax.ShapeDtypeStruct((n_pair, chunks, 2 * CHUNK, col_pad), BF16),
            jax.ShapeDtypeStruct((n_pair, chunks, 2 * CHUNK, row_pad), BF16),
        ],
        in_specs=[vmem] * len(args) + [pl.BlockSpec(memory_space=pl.ANY)] * len(large),
        out_specs=[vmem] * 2,
        scratch_shapes=[pltpu.VMEM(x.shape, x.dtype) for x in large] + [
            pltpu.VMEM((n_group, *tile_info.shape), jnp.int32),
            pltpu.VMEM((half, GRID * GRID), BF16),
            pltpu.VMEM((half, GRID * GRID), BF16),
            pltpu.VMEM((2 * half, width), BF16),
            pltpu.VMEM((2 * half, width), BF16),
            pltpu.VMEM((chunks, height, width), BF16),
            pltpu.VMEM((n_pair, chunks, 2 * CHUNK, row_pad), BF16),
            dma((len(large),)),
            dma((n_group,)), dma((n_group,)),
            dma((n_pair // 2,)), dma((n_pair // 2,)),
            dma((n_pair // 2,)), dma((n_pair // 2,)),
            dma((n_pair,)), dma((n_pair,)),
        ],
        compiler_params=pltpu.CompilerParams(
            collective_id=0, has_side_effects=True, vmem_limit_bytes=56 * 2**20
        ),
    )(*args, *large)


def product_kernel(scale, rows, cols, out):
    value = lax.dot_general(
        rows[...], cols[...], (((0,), (0,)), ((), ())), preferred_element_type=F32
    )
    out[...] = value[: out.shape[0], : out.shape[1]] * scale


def product(rows, cols, n_rows, n_cols, scale):
    depth, row_pad = rows.shape
    block = LANES if n_rows % LANES == 0 else n_rows
    return pl.pallas_call(
        functools.partial(product_kernel, scale),
        grid=(n_rows // block,),
        out_shape=jax.ShapeDtypeStruct((n_rows, n_cols), F32),
        in_specs=[
            pl.BlockSpec((depth, pad_to(block, LANES)), lambda n: (0, n)),
            pl.BlockSpec(cols.shape, lambda n: (0, 0)),
        ],
        out_specs=pl.BlockSpec((block, n_cols), lambda n: (n, 0)),
        compiler_params=pltpu.CompilerParams(vmem_limit_bytes=48 * 2**20),
    )(rows, cols)


def local(
    valence,
    conduction,
    valence_energy,
    conduction_energy,
    pair_valence,
    pair_conduction,
    pair_count,
    g_index,
):
    slot_count = pair_valence.shape[0]
    total_g = g_index.shape[0]
    n_pair = lax.axis_size("pair")
    n_grow = lax.axis_size("grow")
    n_gcol = lax.axis_size("gcol")
    sub_rows = total_g // (n_pair * n_grow)
    col_width = total_g // n_gcol
    row_pad, col_pad = pad_to(sub_rows, LANES), pad_to(col_width, LANES)
    live = (jnp.arange(slot_count, dtype=jnp.int32) < pair_count[0]).astype(jnp.int32)
    info = jnp.stack([pair_valence, pair_conduction, live], axis=1)
    info = jnp.pad(jnp.tile(info, (CHUNK // slot_count, 1)), ((0, 0), (0, LANES - 3)))
    if row_pad == sub_rows and col_pad == col_width:
        g_list = g_index[None, :]
        col_at = lambda gcol: gcol * col_width
        row_at = lambda pair, grow: (pair * n_grow + grow) * sub_rows
    else:
        by_col = jnp.pad(g_index.reshape(n_gcol, col_width), ((0, 0), (0, col_pad - col_width)))
        by_row = jnp.pad(g_index.reshape(-1, sub_rows), ((0, 0), (0, row_pad - sub_rows)))
        g_list = jnp.concatenate([by_col.reshape(-1), by_row.reshape(-1)])[None, :]
        col_at = lambda gcol: gcol * col_pad
        row_at = lambda pair, grow: n_gcol * col_pad + (pair * n_grow + grow) * row_pad
    chunks = slot_count * n_grow * n_gcol // CHUNK
    layout = (n_pair, n_grow, n_gcol, slot_count, chunks, col_at, row_at)
    cols, rows = panels(
        info, valence_energy[None, :], conduction_energy[None, :], g_list,
        valence, conduction, total_g, col_pad, row_pad, layout,
    )
    total_slots = slot_count * n_pair * n_grow * n_gcol
    return product(
        rows.reshape(-1, row_pad), cols.reshape(-1, col_pad), sub_rows, col_width,
        -1.0 / math.sqrt(total_slots),
    )


def solution(mesh):
    return jax.shard_map(
        local,
        mesh=mesh,
        in_specs=(
            P(),
            P("pair", None),
            P(),
            P("pair"),
            P(("pair", "grow", "gcol")),
            P(("pair", "grow", "gcol")),
            P(("pair", "grow", "gcol")),
            P(),
        ),
        out_specs=P(("pair", "grow"), "gcol"),
        check_vma=False,
    )
```

```python
import functools
import math

import jax
import jax.numpy as jnp
import ml_dtypes
import numpy as np
from jax import lax
from jax.experimental import pallas as pl
from jax.experimental.pallas import tpu as pltpu
from jax.sharding import PartitionSpec as P

GRID = 32
CHUNK = 16
LANES = 128
TILE = 256
MAIN = 256
MESH = pl.DeviceIdType.MESH
BF16 = jnp.bfloat16
F32 = jnp.float32


def pad_to(size, unit):
    return -(-size // unit) * unit


def ball(total_g):
    freq = np.arange(-(GRID // 2) + 1, GRID // 2)
    square = freq[:, None, None] ** 2 + freq[None, :, None] ** 2 + freq[None, None, :] ** 2
    return int(np.sort(square.ravel())[total_g])


def split(values):
    high = values.astype(ml_dtypes.bfloat16)
    low = (values - high.astype(np.float64)).astype(ml_dtypes.bfloat16)
    return high, low


def tables(total_g):
    limit = ball(total_g)
    reach = math.isqrt(limit)
    plane = []
    for b in range(0, reach + 1):
        for c in range(-reach, reach + 1):
            if b * b + c * c <= limit and (b > 0 or c >= 0):
                plane.append((b * b + c * c, b, c))
    plane.sort()
    extra = plane[MAIN:]
    short = math.isqrt(limit - extra[0][0]) if extra else -1
    width = pad_to(len(plane), LANES)
    keys = np.full((width,), -1, np.int32)
    bs = np.zeros((width,), np.int64)
    cs = np.zeros((width,), np.int64)
    for at, (_, b, c) in enumerate(plane):
        keys[at] = b * GRID + c + GRID // 2
        bs[at], cs[at] = b, c
    cell = np.arange(GRID * GRID)
    phase = (cell[:, None] // GRID * bs[None] + cell[:, None] % GRID * cs[None]) % GRID
    angle = phase * (2.0 * math.pi / GRID)
    used = keys[None] >= 0
    first = np.concatenate([np.cos(angle) * used, -np.sin(angle) * used], axis=1)
    points = np.arange(1, GRID // 2 + 1)
    angle = (np.arange(reach + 1)[:, None] * points[None] % GRID) * (2.0 * math.pi / GRID)
    second = np.stack([np.cos(angle), np.sin(angle)])
    second = np.kron(second, np.eye(CHUNK)[None])
    keys = np.repeat(keys[:, None], TILE, axis=1)
    return reach, short, width, keys, split(first), split(second)


def body(
    reach, short, width, layout,
    tile_info, energy_v, energy_c, g_list, keys, valence_in, conduction_in, *refs,
):
    n_pair, n_grow, n_gcol, per_device, chunks, col_at, row_at = layout
    tables_in, (cols, rows), scratch = refs[:4], refs[4:6], refs[6:]
    bands, first_h, first_l, second_h, second_l = scratch[:5]
    infos, dens_h, dens_l, even_h, even_l, odd_h, odd_l, spec, row_buf = scratch[5:14]
    load_sem, info_send, info_recv, col_send, col_recv, relay_send, relay_recv, row_send, row_recv = scratch[14:]
    n_v, n_c = valence_in.shape[0], conduction_in.shape[0]

    me, grow, gcol = lax.axis_index("pair"), lax.axis_index("grow"), lax.axis_index("gcol")
    chip, core = me // 2, me % 2
    n_chip, n_group = n_pair // 2, n_grow * n_gcol
    group = grow * n_gcol + gcol
    sibling = {"pair": chip * 2 + (1 - core)}

    def group_id(step):
        other = (group + step) % n_group
        return {"grow": other // n_gcol, "gcol": other % n_gcol}

    def pair_at(step):
        return (chip + 1 + step // 2) % n_chip * 2 + (core + step % 2) % 2

    own_step = (n_chip - 1) * 2

    loads = [
        pltpu.make_async_copy(source, target, load_sem.at[n])
        for n, (source, target) in enumerate(
            zip(
                (valence_in, conduction_in, *tables_in),
                (bands.at[pl.ds(0, n_v)], bands.at[pl.ds(n_v, n_c)], *scratch[1:5]),
            )
        )
    ]
    for load in loads:
        load.start()

    barrier = pltpu.get_barrier_semaphore()

    def greet_group(step, carry):
        pl.semaphore_signal(barrier, inc=1, device_id=group_id(step), device_id_type=MESH)
        return carry

    def greet_pair(step, carry):
        @pl.when(step != own_step)
        def _():
            pl.semaphore_signal(
                barrier, inc=1, device_id={"pair": pair_at(step)}, device_id_type=MESH
            )
        return carry

    lax.fori_loop(1, n_group, greet_group, 0)
    lax.fori_loop(0, n_pair, greet_pair, 0)
    pl.semaphore_wait(barrier, n_group - 1 + n_pair - 1)

    def info_copy(step):
        return pltpu.make_async_remote_copy(
            src_ref=tile_info, dst_ref=infos.at[group],
            send_sem=info_send.at[step], recv_sem=info_recv.at[step],
            device_id=group_id(step), device_id_type=MESH,
        )

    def start_info(step, carry):
        info_copy(step).start()
        return carry

    def wait_info(step, carry):
        info_copy(step).wait()
        return carry

    lax.fori_loop(1, n_group, start_info, 0)
    infos[group] = tile_info[...]
    lax.fori_loop(1, n_group, wait_info, 0)

    plane = GRID * GRID
    together = CHUNK // per_device
    dot = functools.partial(jnp.dot, preferred_element_type=F32)
    loads[0].wait()
    loads[1].wait()

    def transform(n, first_chunk):
        slot = lax.broadcasted_iota(jnp.int32, (CHUNK, LANES), 0)
        info = jnp.zeros((CHUNK, LANES), jnp.int32)
        for d in range(together):
            info = jnp.where(slot // per_device == d, infos[n * together + d], info)
        pick_v = info[:, 0:1] == lax.broadcasted_iota(jnp.int32, (CHUNK, n_v), 1)
        pick_c = info[:, 1:2] == lax.broadcasted_iota(jnp.int32, (CHUNK, n_c), 1)
        live = info[:, 2:3].astype(F32)
        gap = jnp.sum(jnp.where(pick_c, energy_c[...], 0.0), axis=1, keepdims=True) - jnp.sum(
            jnp.where(pick_v, energy_v[...], 0.0), axis=1, keepdims=True
        )
        factor = live * jnp.sqrt(4.0 / gap) / math.sqrt(GRID**3)
        band = lax.broadcasted_iota(jnp.int32, (CHUNK, n_v + n_c), 1)
        hot = jnp.concatenate(
            [jnp.where(info[:, 0:1] == band, 1.0, 0.0), jnp.where(info[:, 1:2] + n_v == band, 1.0, 0.0)],
            axis=0,
        ).astype(BF16)
        for i in range(GRID):
            at = slice(i * plane, (i + 1) * plane)
            both = dot(hot, bands[:, at])
            dens = both[:CHUNK] * both[CHUNK:]
            high = dens.astype(BF16)
            span = slice(i * CHUNK, (i + 1) * CHUNK)
            dens_h[span, :] = high
            dens_l[span, :] = (dens - high.astype(F32)).astype(BF16)
        if first_chunk:
            loads[2].wait()
            loads[3].wait()
        middle = GRID // 2
        start = []
        for part in range(2):
            at = slice(part * width, (part + 1) * width)
            value = (
                dot(dens_h[...], first_h[:, at])
                + dot(dens_l[...], first_h[:, at])
                + dot(dens_h[...], first_l[:, at])
            ).reshape(GRID, CHUNK, width)
            start.append(value[0])
            for i in range(1, middle + 1):
                span = slice((i - 1) * CHUNK, i * CHUNK)
                even, odd = value[i], jnp.zeros((CHUNK, width), F32)
                if i < middle:
                    even, odd = value[i] + value[GRID - i], value[i] - value[GRID - i]
                for whole, top, rest in ((even, even_h, even_l), (odd, odd_h, odd_l)):
                    high = whole.astype(BF16)
                    top[span, at] = high
                    rest[span, at] = (whole - high.astype(F32)).astype(BF16)
        if first_chunk:
            loads[4].wait()
            loads[5].wait()
        both = []
        for which, top, rest in ((0, even_h, even_l), (1, odd_h, odd_l)):
            value = (
                dot(second_h[which], top[...])
                + dot(second_h[which], rest[...])
                + dot(second_l[which], top[...])
            )
            both.append(value.reshape(reach + 1, CHUNK, 2 * width))
        even, odd = both
        for a in range(reach + 1):
            even_r, even_i = even[a, :, :width] + start[0], even[a, :, width:] + start[1]
            odd_r, odd_i = odd[a, :, :width], odd[a, :, width:]
            parts = [(reach + a, even_r + odd_i, even_i - odd_r)]
            if a:
                parts.append((reach - a, even_r - odd_i, even_i + odd_r))
            for at, real, imag in parts:
                at = 2 * CHUNK * at
                spec[n, at:at + CHUNK, :] = (real * factor).astype(BF16)
                spec[n, at + CHUNK:at + 2 * CHUNK, :] = (imag * factor).astype(BF16)

    transform(0, True)
    if chunks > 1:
        @pl.loop(1, chunks)
        def _(n):
            transform(n, False)

    height = 2 * CHUNK
    low, high = (reach - short) * height, (reach + short + 1) * height

    def select(n, source, size, out, target):
        cell = g_list[:, pl.ds(pl.multiple_of(source, LANES), size)]
        centre = lambda v: jnp.where(v < GRID // 2, v, v - GRID)
        a = centre(cell // (GRID * GRID))
        b = centre(cell // GRID % GRID)
        c = centre(cell % GRID)
        flip = (b < 0) | ((b == 0) & (c < 0))
        a = jnp.where(flip, -a, a)
        b = jnp.where(flip, -b, b)
        c = jnp.where(flip, -c, c)
        key = b * GRID + c + GRID // 2
        hot = jnp.where(keys[:, :size] == key, 1.0, 0.0).astype(BF16)
        picked = dot(spec[n, :, :MAIN], hot[:MAIN])
        if width > MAIN:
            more = dot(spec[n, low:high, MAIN:], hot[MAIN:])
        total = jnp.zeros((height, size), F32)
        for k in range(2 * reach + 1):
            value = picked[k * height:(k + 1) * height]
            if width > MAIN and low <= k * height < high:
                value = value + more[k * height - low:(k + 1) * height - low]
            total = jnp.where(a == k - reach, value, total)
        imag = total[CHUNK:]
        at = pl.ds(target, size)
        out[n, :CHUNK, at] = total[:CHUNK].astype(BF16)
        out[n, CHUNK:, at] = jnp.where(flip, -imag, imag).astype(BF16)

    def block(source, size, out):
        for n in range(chunks) if chunks == 1 else [None]:
            def run(n):
                @pl.loop(0, size // TILE)
                def _(t):
                    select(n, source + t * TILE, TILE, out, pl.multiple_of(t * TILE, TILE))
                if size % TILE:
                    done = size // TILE * TILE
                    select(n, source + done, size - done, out, done)
            if n is None:
                pl.loop(0, chunks)(run)
            else:
                run(n)

    def col_copy(step):
        peer = (chip + step) % n_chip * 2 + core
        return pltpu.make_async_remote_copy(
            src_ref=cols.at[me], dst_ref=cols.at[me],
            send_sem=col_send.at[step], recv_sem=col_recv.at[step],
            device_id=sibling if step == 0 else {"pair": peer}, device_id_type=MESH,
        )

    def relay_copy(step):
        source = (chip + n_chip - step) % n_chip * 2 + core
        return pltpu.make_async_remote_copy(
            src_ref=cols.at[source], dst_ref=cols.at[source],
            send_sem=relay_send.at[step], recv_sem=relay_recv.at[step],
            device_id=sibling, device_id_type=MESH,
        )

    def row_copy(step):
        return pltpu.make_async_remote_copy(
            src_ref=row_buf.at[step], dst_ref=rows.at[me],
            send_sem=row_send.at[step], recv_sem=row_recv.at[step],
            device_id={"pair": pair_at(step)}, device_id_type=MESH,
        )

    block(col_at(gcol), cols.shape[-1], cols.at[me])
    for step in (*range(1, n_chip), 0):
        col_copy(step).start()

    def row_step(step, carry):
        block(row_at(pair_at(step), grow), rows.shape[-1], row_buf.at[step])

        @pl.when(step != own_step)
        def _():
            row_copy(step).start()
        return carry

    lax.fori_loop(0, own_step, row_step, 0)
    for step in range(1, n_chip):
        col_copy(step).wait_recv()
        relay_copy(step).start()
    lax.fori_loop(own_step, n_pair, row_step, 0)
    rows[me] = row_buf[own_step]

    for step in range(1, n_chip):
        col_copy(step).wait_send()
        relay_copy(step).wait()
    col_copy(0).wait()

    def row_wait(step, carry):
        @pl.when(step != own_step)
        def _():
            row_copy(step).wait()
        return carry

    lax.fori_loop(0, n_pair, row_wait, 0)


def panels(tile_info, energy_v, energy_c, g_list, valence, conduction, total_g, col_pad, row_pad, layout):
    reach, short, width, keys, first, second = tables(total_g)
    n_pair, n_grow, n_gcol, per_device, chunks = layout[:5]
    consts = [jnp.asarray(x) for x in (*first, *second)]
    large = [valence, conduction, *consts]
    args = [tile_info, energy_v, energy_c, g_list, jnp.asarray(keys)]
    height = 2 * CHUNK * (2 * reach + 1)
    half = GRID * CHUNK
    n_group = n_grow * n_gcol
    n_v, n_c = valence.shape[0], conduction.shape[0]
    vmem = pl.BlockSpec(memory_space=pltpu.VMEM)
    dma = pltpu.SemaphoreType.DMA
    return pl.pallas_call(
        functools.partial(body, reach, short, width, layout),
        out_shape=[
            jax.ShapeDtypeStruct((n_pair, chunks, 2 * CHUNK, col_pad), BF16),
            jax.ShapeDtypeStruct((n_pair, chunks, 2 * CHUNK, row_pad), BF16),
        ],
        in_specs=[vmem] * len(args) + [pl.BlockSpec(memory_space=pl.ANY)] * len(large),
        out_specs=[vmem] * 2,
        scratch_shapes=[pltpu.VMEM((n_v + n_c, GRID**3), BF16)]
        + [pltpu.VMEM(x.shape, x.dtype) for x in consts] + [
            pltpu.VMEM((n_group, *tile_info.shape), jnp.int32),
            pltpu.VMEM((half, GRID * GRID), BF16),
            pltpu.VMEM((half, GRID * GRID), BF16),
            *[pltpu.VMEM((half // 2, 2 * width), BF16)] * 4,
            pltpu.VMEM((chunks, height, width), BF16),
            pltpu.VMEM((n_pair, chunks, 2 * CHUNK, row_pad), BF16),
            dma((len(large),)),
            dma((n_group,)), dma((n_group,)),
            dma((n_pair // 2,)), dma((n_pair // 2,)),
            dma((n_pair // 2,)), dma((n_pair // 2,)),
            dma((n_pair,)), dma((n_pair,)),
        ],
        compiler_params=pltpu.CompilerParams(
            collective_id=0, has_side_effects=True, vmem_limit_bytes=56 * 2**20
        ),
    )(*args, *large)


def product_kernel(scale, rows, cols, out, turned):
    @pl.when(pl.program_id(0) == 0)
    def _():
        turned[...] = rows[...].T

    value = jnp.dot(turned[...], cols[...], preferred_element_type=F32)
    out[...] = value[: out.shape[0]] * scale


def product(rows, cols, n_rows, n_cols, scale):
    depth, row_pad = rows.shape
    block = TILE if n_cols % TILE == 0 else LANES
    return pl.pallas_call(
        functools.partial(product_kernel, scale),
        grid=(n_cols // block,),
        out_shape=jax.ShapeDtypeStruct((n_rows, n_cols), F32),
        in_specs=[
            pl.BlockSpec((depth, row_pad), lambda n: (0, 0)),
            pl.BlockSpec((depth, block), lambda n: (0, n)),
        ],
        out_specs=pl.BlockSpec((n_rows, block), lambda n: (0, n)),
        scratch_shapes=[pltpu.VMEM((row_pad, depth), BF16)],
        compiler_params=pltpu.CompilerParams(vmem_limit_bytes=62 * 2**20),
    )(rows, cols)


def local(
    valence,
    conduction,
    valence_energy,
    conduction_energy,
    pair_valence,
    pair_conduction,
    pair_count,
    g_index,
):
    slot_count = pair_valence.shape[0]
    total_g = g_index.shape[0]
    n_pair = lax.axis_size("pair")
    n_grow = lax.axis_size("grow")
    n_gcol = lax.axis_size("gcol")
    sub_rows = total_g // (n_pair * n_grow)
    col_width = total_g // n_gcol
    row_pad, col_pad = pad_to(sub_rows, LANES), pad_to(col_width, LANES)
    live = (jnp.arange(slot_count, dtype=jnp.int32) < pair_count[0]).astype(jnp.int32)
    info = jnp.stack([pair_valence, pair_conduction, live], axis=1)
    info = jnp.pad(jnp.tile(info, (CHUNK // slot_count, 1)), ((0, 0), (0, LANES - 3)))
    if row_pad == sub_rows and col_pad == col_width:
        g_list = g_index[None, :]
        col_at = lambda gcol: gcol * col_width
        row_at = lambda pair, grow: (pair * n_grow + grow) * sub_rows
    else:
        by_col = jnp.pad(g_index.reshape(n_gcol, col_width), ((0, 0), (0, col_pad - col_width)))
        by_row = jnp.pad(g_index.reshape(-1, sub_rows), ((0, 0), (0, row_pad - sub_rows)))
        g_list = jnp.concatenate([by_col.reshape(-1), by_row.reshape(-1)])[None, :]
        col_at = lambda gcol: gcol * col_pad
        row_at = lambda pair, grow: n_gcol * col_pad + (pair * n_grow + grow) * row_pad
    chunks = slot_count * n_grow * n_gcol // CHUNK
    layout = (n_pair, n_grow, n_gcol, slot_count, chunks, col_at, row_at)
    cols, rows = panels(
        info, valence_energy[None, :], conduction_energy[None, :], g_list,
        valence, conduction, total_g, col_pad, row_pad, layout,
    )
    total_slots = slot_count * n_pair * n_grow * n_gcol
    return product(
        rows.reshape(-1, row_pad), cols.reshape(-1, col_pad), sub_rows, col_width,
        -1.0 / math.sqrt(total_slots),
    )


def solution(mesh):
    return jax.shard_map(
        local,
        mesh=mesh,
        in_specs=(
            P(),
            P("pair", None),
            P(),
            P("pair"),
            P(("pair", "grow", "gcol")),
            P(("pair", "grow", "gcol")),
            P(("pair", "grow", "gcol")),
            P(),
        ),
        out_specs=P(("pair", "grow"), "gcol"),
        check_vma=False,
    )
```

```python
import functools
import math

import jax
import jax.numpy as jnp
import ml_dtypes
import numpy as np
from jax import lax
from jax.experimental import pallas as pl
from jax.experimental.pallas import tpu as pltpu
from jax.sharding import PartitionSpec as P

GRID = 32
BITS = 5
CHUNK = 16
LANES = 128
TILE = 256
MAIN = 256
PIECE = 1152
MESH = pl.DeviceIdType.MESH
BF16 = jnp.bfloat16
F32 = jnp.float32


def pad_to(size, unit):
    return -(-size // unit) * unit


def ball(total_g):
    freq = np.arange(-(GRID // 2) + 1, GRID // 2)
    square = freq[:, None, None] ** 2 + freq[None, :, None] ** 2 + freq[None, None, :] ** 2
    return int(np.sort(square.ravel())[total_g])


def split(values):
    high = values.astype(ml_dtypes.bfloat16)
    low = (values - high.astype(np.float64)).astype(ml_dtypes.bfloat16)
    return high, low


def tables(total_g):
    limit = ball(total_g)
    reach = math.isqrt(limit)
    plane = []
    for b in range(0, reach + 1):
        for c in range(-reach, reach + 1):
            if b * b + c * c <= limit and (b > 0 or c >= 0):
                plane.append((b * b + c * c, b, c))
    plane.sort()
    extra = plane[MAIN:]
    short = math.isqrt(limit - extra[0][0]) if extra else -1
    width = pad_to(len(plane), LANES)
    keys = np.full((width,), -1, np.int32)
    bs = np.zeros((width,), np.int64)
    cs = np.zeros((width,), np.int64)
    for at, (_, b, c) in enumerate(plane):
        keys[at] = b * GRID + c + GRID // 2
        bs[at], cs[at] = b, c
    cell = np.arange(GRID * GRID)
    phase = (cell[:, None] // GRID * bs[None] + cell[:, None] % GRID * cs[None]) % GRID
    angle = phase * (2.0 * math.pi / GRID)
    used = keys[None] >= 0
    first = np.concatenate([np.cos(angle) * used, -np.sin(angle) * used], axis=1)
    points = np.arange(1, GRID // 2 + 1)
    angle = (np.arange(reach + 1)[:, None] * points[None] % GRID) * (2.0 * math.pi / GRID)
    second = np.stack([np.cos(angle), np.sin(angle)])
    second = np.kron(second, np.eye(CHUNK)[None])
    keys = np.repeat(keys[: pad_to(len(plane), CHUNK), None], TILE, axis=1)
    return reach, short, width, keys, split(first), split(second)


def body(
    reach, short, width, layout,
    ids_v, ids_c, count, energy_v, energy_c, g_list, keys, valence_in, conduction_in, *refs,
):
    n_pair, n_grow, n_gcol, per_device, chunks, col_at, row_at = layout
    tables_in, (cols, rows), scratch = refs[:4], refs[4:6], refs[6:]
    bands, first_h, first_l, second_h, second_l = scratch[:5]
    infos, dens_h, dens_l, even_h, even_l, odd_h, odd_l, spec, row_buf = scratch[5:14]
    tile_info = infos.at[n_grow * n_gcol]
    load_sem, info_send, info_recv, col_send, col_recv, relay_send, relay_recv, row_send, row_recv = scratch[14:]
    n_v, n_c = valence_in.shape[0], conduction_in.shape[0]

    me, grow, gcol = lax.axis_index("pair"), lax.axis_index("grow"), lax.axis_index("gcol")
    chip, core = me // 2, me % 2
    n_chip, n_group = n_pair // 2, n_grow * n_gcol
    group = grow * n_gcol + gcol
    sibling = {"pair": chip * 2 + (1 - core)}

    def group_id(step):
        other = (group + step) % n_group
        return {"grow": other // n_gcol, "gcol": other % n_gcol}

    def pair_at(step):
        return (chip + 1 + step // 2) % n_chip * 2 + (core + step % 2) % 2

    own_step = (n_chip - 1) * 2

    loads = [
        pltpu.make_async_copy(source, target, load_sem.at[n])
        for n, (source, target) in enumerate(
            zip(
                (valence_in, conduction_in, *tables_in),
                (bands.at[pl.ds(0, n_v)], bands.at[pl.ds(n_v, n_c)], *scratch[1:5]),
            )
        )
    ]
    for load in loads:
        load.start()

    slot = lax.broadcasted_iota(jnp.int32, (CHUNK, LANES), 0) % per_device
    lane = lax.broadcasted_iota(jnp.int32, (CHUNK, LANES), 1)
    mine = jnp.zeros((CHUNK, LANES), jnp.int32)
    for j in range(per_device):
        live = jnp.where(count[0] > j, 1, 0)
        row = jnp.where(lane == 0, ids_v[j], jnp.where(lane == 1, ids_c[j], live))
        mine = jnp.where(slot == j, row, mine)
    tile_info[...] = mine

    barrier = pltpu.get_barrier_semaphore()

    def greet_group(step, carry):
        pl.semaphore_signal(barrier, inc=1, device_id=group_id(step), device_id_type=MESH)
        return carry

    def greet_pair(step, carry):
        @pl.when(step != own_step)
        def _():
            pl.semaphore_signal(
                barrier, inc=1, device_id={"pair": pair_at(step)}, device_id_type=MESH
            )
        return carry

    lax.fori_loop(1, n_group, greet_group, 0)
    lax.fori_loop(0, n_pair, greet_pair, 0)
    pl.semaphore_wait(barrier, n_group - 1 + n_pair - 1)

    def info_copy(step):
        return pltpu.make_async_remote_copy(
            src_ref=tile_info, dst_ref=infos.at[group],
            send_sem=info_send.at[step], recv_sem=info_recv.at[step],
            device_id=group_id(step), device_id_type=MESH,
        )

    def start_info(step, carry):
        info_copy(step).start()
        return carry

    def wait_info(step, carry):
        info_copy(step).wait()
        return carry

    lax.fori_loop(1, n_group, start_info, 0)
    infos[group] = mine
    lax.fori_loop(1, n_group, wait_info, 0)

    plane = GRID * GRID
    together = CHUNK // per_device
    dot = functools.partial(jnp.dot, preferred_element_type=F32)
    loads[0].wait()
    loads[1].wait()

    def transform(n, first_chunk):
        slot = lax.broadcasted_iota(jnp.int32, (CHUNK, LANES), 0)
        info = jnp.zeros((CHUNK, LANES), jnp.int32)
        for d in range(together):
            info = jnp.where(slot // per_device == d, infos[n * together + d], info)
        pick_v = info[:, 0:1] == lax.broadcasted_iota(jnp.int32, (CHUNK, n_v), 1)
        pick_c = info[:, 1:2] == lax.broadcasted_iota(jnp.int32, (CHUNK, n_c), 1)
        live = info[:, 2:3].astype(F32)
        gap = jnp.sum(jnp.where(pick_c, energy_c[...], 0.0), axis=1, keepdims=True) - jnp.sum(
            jnp.where(pick_v, energy_v[...], 0.0), axis=1, keepdims=True
        )
        factor = live * jnp.sqrt(4.0 / gap) / math.sqrt(GRID**3)
        band = lax.broadcasted_iota(jnp.int32, (CHUNK, n_v + n_c), 1)
        hot = jnp.concatenate(
            [jnp.where(info[:, 0:1] == band, 1.0, 0.0), jnp.where(info[:, 1:2] + n_v == band, 1.0, 0.0)],
            axis=0,
        ).astype(BF16)
        for i in range(GRID):
            at = slice(i * plane, (i + 1) * plane)
            both = dot(hot, bands[:, at])
            dens = both[:CHUNK] * both[CHUNK:]
            high = dens.astype(BF16)
            span = slice(i * CHUNK, (i + 1) * CHUNK)
            dens_h[span, :] = high
            dens_l[span, :] = (dens - high.astype(F32)).astype(BF16)
        if first_chunk:
            loads[2].wait()
            loads[3].wait()
        middle = GRID // 2
        start = []
        for part in range(2):
            at = slice(part * width, (part + 1) * width)
            value = (
                dot(dens_h[...], first_h[:, at])
                + dot(dens_l[...], first_h[:, at])
                + dot(dens_h[...], first_l[:, at])
            ).reshape(GRID, CHUNK, width)
            start.append(value[0])
            for i in range(1, middle + 1):
                span = slice((i - 1) * CHUNK, i * CHUNK)
                even, odd = value[i], jnp.zeros((CHUNK, width), F32)
                if i < middle:
                    even, odd = value[i] + value[GRID - i], value[i] - value[GRID - i]
                for whole, top, rest in ((even, even_h, even_l), (odd, odd_h, odd_l)):
                    high = whole.astype(BF16)
                    top[span, at] = high
                    rest[span, at] = (whole - high.astype(F32)).astype(BF16)
        if first_chunk:
            loads[4].wait()
            loads[5].wait()
        both = []
        for which, top, rest in ((0, even_h, even_l), (1, odd_h, odd_l)):
            value = (
                dot(second_h[which], top[...])
                + dot(second_h[which], rest[...])
                + dot(second_l[which], top[...])
            )
            both.append(value.reshape(reach + 1, CHUNK, 2 * width))
        even, odd = both
        for a in range(reach + 1):
            even_r, even_i = even[a, :, :width] + start[0], even[a, :, width:] + start[1]
            odd_r, odd_i = odd[a, :, :width], odd[a, :, width:]
            parts = [(reach + a, even_r + odd_i, even_i - odd_r)]
            if a:
                parts.append((reach - a, even_r - odd_i, even_i + odd_r))
            for at, real, imag in parts:
                at = 2 * CHUNK * at
                spec[n, at:at + CHUNK, :] = (real * factor).astype(BF16)
                spec[n, at + CHUNK:at + 2 * CHUNK, :] = (imag * factor).astype(BF16)

    transform(0, True)
    if chunks > 1:
        @pl.loop(1, chunks)
        def _(n):
            transform(n, False)

    height = 2 * CHUNK
    low, high = (reach - short) * height, (reach + short + 1) * height

    def select(n, source, size, out, target):
        cell = g_list[:, pl.ds(pl.multiple_of(source, LANES), size)]
        centre = lambda v: jnp.where(v < GRID // 2, v, v - GRID)
        a = centre(cell >> (2 * BITS))
        b = centre((cell >> BITS) & (GRID - 1))
        c = centre(cell & (GRID - 1))
        flip = (b < 0) | ((b == 0) & (c < 0))
        a = jnp.where(flip, -a, a)
        b = jnp.where(flip, -b, b)
        c = jnp.where(flip, -c, c)
        key = b * GRID + c + GRID // 2
        hot = jnp.where(keys[:, :size] == key, 1.0, 0.0).astype(BF16)
        picked = dot(spec[n, :, :MAIN], hot[:MAIN])
        if width > MAIN:
            more = dot(spec[n, low:high, MAIN:keys.shape[0]], hot[MAIN:])
        total = jnp.zeros((height, size), F32)
        for k in range(2 * reach + 1):
            value = picked[k * height:(k + 1) * height]
            if width > MAIN and low <= k * height < high:
                value = value + more[k * height - low:(k + 1) * height - low]
            total = jnp.where(a == k - reach, value, total)
        imag = total[CHUNK:]
        at = pl.ds(target, size)
        out[n, :CHUNK, at] = total[:CHUNK].astype(BF16)
        out[n, CHUNK:, at] = jnp.where(flip, -imag, imag).astype(BF16)

    def block(source, size, out):
        piece = max(x for x in range(LANES, PIECE + 1, LANES) if size % x == 0)

        def run(n):
            def part(t):
                for done in range(0, piece, TILE):
                    at = t * piece + done
                    at = at if isinstance(at, int) else pl.multiple_of(at, LANES)
                    select(n, source + at, min(TILE, piece - done), out, at)

            if size == piece:
                part(0)
            else:
                pl.loop(0, size // piece)(part)

        if chunks == 1:
            run(0)
        else:
            pl.loop(0, chunks)(run)

    def col_copy(step):
        peer = (chip + step) % n_chip * 2 + core
        return pltpu.make_async_remote_copy(
            src_ref=cols.at[me], dst_ref=cols.at[me],
            send_sem=col_send.at[step], recv_sem=col_recv.at[step],
            device_id=sibling if step == 0 else {"pair": peer}, device_id_type=MESH,
        )

    def relay_copy(step):
        source = (chip + n_chip - step) % n_chip * 2 + core
        return pltpu.make_async_remote_copy(
            src_ref=cols.at[source], dst_ref=cols.at[source],
            send_sem=relay_send.at[step], recv_sem=relay_recv.at[step],
            device_id=sibling, device_id_type=MESH,
        )

    def row_copy(step):
        return pltpu.make_async_remote_copy(
            src_ref=row_buf.at[step], dst_ref=rows.at[me],
            send_sem=row_send.at[step], recv_sem=row_recv.at[step],
            device_id={"pair": pair_at(step)}, device_id_type=MESH,
        )

    block(col_at(gcol), cols.shape[-1], cols.at[me])
    for step in (*range(1, n_chip), 0):
        col_copy(step).start()

    def row_step(step, carry):
        block(row_at(pair_at(step), grow), rows.shape[-1], row_buf.at[step])

        @pl.when(step != own_step)
        def _():
            row_copy(step).start()
        return carry

    lax.fori_loop(0, own_step, row_step, 0)
    for step in range(1, n_chip):
        col_copy(step).wait_recv()
        relay_copy(step).start()
    lax.fori_loop(own_step, n_pair, row_step, 0)
    rows[me] = row_buf[own_step]

    for step in range(1, n_chip):
        col_copy(step).wait_send()
        relay_copy(step).wait()
    col_copy(0).wait()

    def row_wait(step, carry):
        @pl.when(step != own_step)
        def _():
            row_copy(step).wait()
        return carry

    lax.fori_loop(0, n_pair, row_wait, 0)


def panels(ids, energy_v, energy_c, g_list, valence, conduction, total_g, col_pad, row_pad, layout):
    reach, short, width, keys, first, second = tables(total_g)
    n_pair, n_grow, n_gcol, per_device, chunks = layout[:5]
    consts = [jnp.asarray(x) for x in (*first, *second)]
    large = [valence, conduction, *consts]
    args = [energy_v, energy_c, g_list, jnp.asarray(keys)]
    height = 2 * CHUNK * (2 * reach + 1)
    half = GRID * CHUNK
    n_group = n_grow * n_gcol
    n_v, n_c = valence.shape[0], conduction.shape[0]
    vmem = pl.BlockSpec(memory_space=pltpu.VMEM)
    dma = pltpu.SemaphoreType.DMA
    return pl.pallas_call(
        functools.partial(body, reach, short, width, layout),
        out_shape=[
            jax.ShapeDtypeStruct((n_pair, chunks, 2 * CHUNK, col_pad), BF16),
            jax.ShapeDtypeStruct((n_pair, chunks, 2 * CHUNK, row_pad), BF16),
        ],
        in_specs=[pl.BlockSpec(memory_space=pltpu.SMEM)] * len(ids) + [vmem] * len(args)
        + [pl.BlockSpec(memory_space=pl.ANY)] * len(large),
        out_specs=[vmem] * 2,
        scratch_shapes=[pltpu.VMEM((n_v + n_c, GRID**3), BF16)]
        + [pltpu.VMEM(x.shape, x.dtype) for x in consts] + [
            pltpu.VMEM((n_group + 1, CHUNK, LANES), jnp.int32),
            pltpu.VMEM((half, GRID * GRID), BF16),
            pltpu.VMEM((half, GRID * GRID), BF16),
            *[pltpu.VMEM((half // 2, 2 * width), BF16)] * 4,
            pltpu.VMEM((chunks, height, width), BF16),
            pltpu.VMEM((n_pair, chunks, 2 * CHUNK, row_pad), BF16),
            dma((len(large),)),
            dma((n_group,)), dma((n_group,)),
            dma((n_pair // 2,)), dma((n_pair // 2,)),
            dma((n_pair // 2,)), dma((n_pair // 2,)),
            dma((n_pair,)), dma((n_pair,)),
        ],
        compiler_params=pltpu.CompilerParams(
            collective_id=0, has_side_effects=True, vmem_limit_bytes=56 * 2**20
        ),
    )(*ids, *args, *large)


def product_kernel(scale, pieces, rows, cols, out, turned, held, sem):
    turned[...] = rows[...].T
    step = out.shape[0] // pieces
    copies = []
    for n in range(pieces):
        at = pl.ds(n * step, step)
        held[at, :] = jnp.dot(turned[at, :], cols[...], preferred_element_type=F32) * scale
        copies.append(pltpu.make_async_copy(held.at[at], out.at[at], sem.at[n]))
        copies[-1].start()
    for copy in copies:
        copy.wait()


def product(rows, cols, n_rows, n_cols, scale):
    depth, row_pad = rows.shape
    pieces = max(x for x in range(1, 9) if n_rows % (16 * x) == 0)
    return pl.pallas_call(
        functools.partial(product_kernel, scale, pieces),
        out_shape=jax.ShapeDtypeStruct((n_rows, n_cols), F32),
        in_specs=[pl.BlockSpec(memory_space=pltpu.VMEM)] * 2,
        out_specs=pl.BlockSpec(memory_space=pl.ANY),
        scratch_shapes=[
            pltpu.VMEM((row_pad, depth), BF16),
            pltpu.VMEM((n_rows, n_cols), F32),
            pltpu.SemaphoreType.DMA((pieces,)),
        ],
        compiler_params=pltpu.CompilerParams(vmem_limit_bytes=62 * 2**20),
    )(rows, cols)


def local(
    valence,
    conduction,
    valence_energy,
    conduction_energy,
    pair_valence,
    pair_conduction,
    pair_count,
    g_index,
):
    slot_count = pair_valence.shape[0]
    total_g = g_index.shape[0]
    n_pair = lax.axis_size("pair")
    n_grow = lax.axis_size("grow")
    n_gcol = lax.axis_size("gcol")
    sub_rows = total_g // (n_pair * n_grow)
    col_width = total_g // n_gcol
    row_pad, col_pad = pad_to(sub_rows, LANES), pad_to(col_width, LANES)
    if row_pad == sub_rows and col_pad == col_width:
        g_list = g_index[None, :]
        col_at = lambda gcol: gcol * col_width
        row_at = lambda pair, grow: (pair * n_grow + grow) * sub_rows
    else:
        by_col = jnp.pad(g_index.reshape(n_gcol, col_width), ((0, 0), (0, col_pad - col_width)))
        by_row = jnp.pad(g_index.reshape(-1, sub_rows), ((0, 0), (0, row_pad - sub_rows)))
        g_list = jnp.concatenate([by_col.reshape(-1), by_row.reshape(-1)])[None, :]
        col_at = lambda gcol: gcol * col_pad
        row_at = lambda pair, grow: n_gcol * col_pad + (pair * n_grow + grow) * row_pad
    chunks = slot_count * n_grow * n_gcol // CHUNK
    layout = (n_pair, n_grow, n_gcol, slot_count, chunks, col_at, row_at)
    cols, rows = panels(
        (pair_valence, pair_conduction, pair_count), valence_energy[None, :], conduction_energy[None, :], g_list,
        valence, conduction, total_g, col_pad, row_pad, layout,
    )
    total_slots = slot_count * n_pair * n_grow * n_gcol
    return product(
        rows.reshape(-1, row_pad), cols.reshape(-1, col_pad), sub_rows, col_width,
        -1.0 / math.sqrt(total_slots),
    )


def solution(mesh):
    return jax.shard_map(
        local,
        mesh=mesh,
        in_specs=(
            P(),
            P("pair", None),
            P(),
            P("pair"),
            P(("pair", "grow", "gcol")),
            P(("pair", "grow", "gcol")),
            P(("pair", "grow", "gcol")),
            P(),
        ),
        out_specs=P(("pair", "grow"), "gcol"),
        check_vma=False,
    )
```

```python
import functools
import math

import jax
import jax.numpy as jnp
import ml_dtypes
import numpy as np
from jax import lax
from jax.experimental import pallas as pl
from jax.experimental.pallas import tpu as pltpu
from jax.sharding import PartitionSpec as P

GRID = 32
BITS = 5
CHUNK = 16
LANES = 128
SUBLANES = 8
TILE = 256
MAIN = 256
PIECE = 1152
MESH = pl.DeviceIdType.MESH
BF16 = jnp.bfloat16
F32 = jnp.float32


def pad_to(size, unit):
    return -(-size // unit) * unit


def ball(total_g):
    freq = np.arange(-(GRID // 2) + 1, GRID // 2)
    square = freq[:, None, None] ** 2 + freq[None, :, None] ** 2 + freq[None, None, :] ** 2
    return int(np.sort(square.ravel())[total_g])


def split(values):
    high = values.astype(ml_dtypes.bfloat16)
    low = (values - high.astype(np.float64)).astype(ml_dtypes.bfloat16)
    return high, low


def tables(total_g):
    limit = ball(total_g)
    reach = math.isqrt(limit)
    plane = []
    for b in range(0, reach + 1):
        for c in range(-reach, reach + 1):
            if b * b + c * c <= limit and (b > 0 or c >= 0):
                plane.append((b * b + c * c, b, c))
    plane.sort()
    extra = plane[MAIN:]
    short = math.isqrt(limit - extra[0][0]) if extra else -1
    width = pad_to(len(plane), LANES)
    keys = np.full((width,), -1, np.int32)
    bs = np.zeros((width,), np.int64)
    cs = np.zeros((width,), np.int64)
    for at, (_, b, c) in enumerate(plane):
        keys[at] = b * GRID + c + GRID // 2
        bs[at], cs[at] = b, c
    cell = np.arange(GRID * GRID)
    phase = (cell[:, None] // GRID * bs[None] + cell[:, None] % GRID * cs[None]) % GRID
    angle = phase * (2.0 * math.pi / GRID)
    used = keys[None] >= 0
    first = np.concatenate([np.cos(angle) * used, -np.sin(angle) * used], axis=1)
    points = np.arange(1, GRID // 2 + 1)
    angle = (np.arange(reach + 1)[:, None] * points[None] % GRID) * (2.0 * math.pi / GRID)
    second = np.stack([np.cos(angle), np.sin(angle)])
    second = np.kron(second, np.eye(CHUNK)[None])
    keys = np.repeat(keys[: pad_to(len(plane), CHUNK), None], TILE, axis=1)
    return reach, short, width, keys, split(first), split(second)


def body(
    reach, short, width, layout,
    ids_v, ids_c, count, energy_v, energy_c, g_list, keys, valence_in, conduction_in, *refs,
):
    n_pair, n_grow, n_gcol, per_device, chunks, col_at, row_at = layout
    tables_in, (cols, rows), scratch = refs[:4], refs[4:6], refs[6:]
    bands, first_h, first_l, second_h, second_l = scratch[:5]
    infos, dens_h, dens_l, even_h, even_l, odd_h, odd_l, spec, row_buf, hots, facts = scratch[5:16]
    tile_info = infos.at[n_grow * n_gcol]
    load_sem, info_send, info_recv, col_send, col_recv, relay_send, relay_recv, row_send, row_recv = scratch[16:]
    n_v, n_c = valence_in.shape[0], conduction_in.shape[0]

    me, grow, gcol = lax.axis_index("pair"), lax.axis_index("grow"), lax.axis_index("gcol")
    chip, core = me // 2, me % 2
    n_chip, n_group = n_pair // 2, n_grow * n_gcol
    group = grow * n_gcol + gcol
    sibling = {"pair": chip * 2 + (1 - core)}

    def group_id(step):
        other = (group + step) % n_group
        return {"grow": other // n_gcol, "gcol": other % n_gcol}

    def pair_at(step):
        return (chip + 1 + step // 2) % n_chip * 2 + (core + step % 2) % 2

    own_step = (n_chip - 1) * 2

    loads = [
        pltpu.make_async_copy(source, target, load_sem.at[n])
        for n, (source, target) in enumerate(
            zip(
                (valence_in, conduction_in, *tables_in),
                (bands.at[pl.ds(0, n_v)], bands.at[pl.ds(n_v, n_c)], *scratch[1:5]),
            )
        )
    ]
    for load in loads:
        load.start()

    slot = lax.broadcasted_iota(jnp.int32, (CHUNK, LANES), 0) % per_device
    lane = lax.broadcasted_iota(jnp.int32, (CHUNK, LANES), 1)
    mine = jnp.zeros((CHUNK, LANES), jnp.int32)
    for j in range(per_device):
        live = jnp.where(count[0] > j, 1, 0)
        row = jnp.where(lane == 0, ids_v[j], jnp.where(lane == 1, ids_c[j], live))
        mine = jnp.where(slot == j, row, mine)
    tile_info[...] = mine

    def prepare(source, target, size):
        cell = g_list[:, pl.ds(source, size)]
        cell = jnp.broadcast_to(cell, (SUBLANES, size))
        centre = lambda v: jnp.where(v < GRID // 2, v, v - GRID)
        a = centre(cell >> (2 * BITS))
        b = centre((cell >> BITS) & (GRID - 1))
        c = centre(cell & (GRID - 1))
        flip = (b < 0) | ((b == 0) & (c < 0))
        a = jnp.where(flip, -a, a)
        b = jnp.where(flip, -b, b)
        c = jnp.where(flip, -c, c)
        key = b * GRID + c + GRID // 2
        here = pl.ds(target, size)
        facts[0, :, here] = a.astype(F32)
        facts[1, :, here] = jnp.where(flip, -1.0, 1.0)
        for at in range(0, keys.shape[0], CHUNK):
            match = keys[at:at + CHUNK, :size] == jnp.concatenate([key] * (CHUNK // SUBLANES), axis=0)
            hots[at:at + CHUNK, here] = jnp.where(match, 1.0, 0.0).astype(BF16)

    def prepare_block(source, target, size):
        @pl.loop(0, size // LANES)
        def _(t):
            prepare(
                pl.multiple_of(source + t * LANES, LANES),
                pl.multiple_of(target + t * LANES, LANES), LANES,
            )

    col_pad, row_pad = cols.shape[-1], rows.shape[-1]
    barrier = pltpu.get_barrier_semaphore()

    def greet_group(step, carry):
        pl.semaphore_signal(barrier, inc=1, device_id=group_id(step), device_id_type=MESH)
        return carry

    def greet_pair(step, carry):
        @pl.when(step != own_step)
        def _():
            pl.semaphore_signal(
                barrier, inc=1, device_id={"pair": pair_at(step)}, device_id_type=MESH
            )
        return carry

    lax.fori_loop(1, n_group, greet_group, 0)
    lax.fori_loop(0, n_pair, greet_pair, 0)
    prepare_block(col_at(gcol), 0, col_pad)
    pl.semaphore_wait(barrier, n_group - 1 + n_pair - 1)

    def info_copy(step):
        return pltpu.make_async_remote_copy(
            src_ref=tile_info, dst_ref=infos.at[group],
            send_sem=info_send.at[step], recv_sem=info_recv.at[step],
            device_id=group_id(step), device_id_type=MESH,
        )

    def start_info(step, carry):
        info_copy(step).start()
        return carry

    def wait_info(step, carry):
        info_copy(step).wait()
        return carry

    lax.fori_loop(1, n_group, start_info, 0)
    infos[group] = mine

    @pl.loop(0, n_pair)
    def _(step):
        prepare_block(row_at(pair_at(step), grow), col_pad + step * row_pad, row_pad)

    lax.fori_loop(1, n_group, wait_info, 0)

    plane = GRID * GRID
    together = CHUNK // per_device
    dot = functools.partial(jnp.dot, preferred_element_type=F32)
    loads[0].wait()
    loads[1].wait()

    def transform(n, first_chunk):
        slot = lax.broadcasted_iota(jnp.int32, (CHUNK, LANES), 0)
        info = jnp.zeros((CHUNK, LANES), jnp.int32)
        for d in range(together):
            info = jnp.where(slot // per_device == d, infos[n * together + d], info)
        pick_v = info[:, 0:1] == lax.broadcasted_iota(jnp.int32, (CHUNK, n_v), 1)
        pick_c = info[:, 1:2] == lax.broadcasted_iota(jnp.int32, (CHUNK, n_c), 1)
        live = info[:, 2:3].astype(F32)
        gap = jnp.sum(jnp.where(pick_c, energy_c[...], 0.0), axis=1, keepdims=True) - jnp.sum(
            jnp.where(pick_v, energy_v[...], 0.0), axis=1, keepdims=True
        )
        factor = live * jnp.sqrt(4.0 / gap) / math.sqrt(GRID**3)
        band = lax.broadcasted_iota(jnp.int32, (CHUNK, n_v + n_c), 1)
        hot = jnp.concatenate(
            [jnp.where(info[:, 0:1] == band, 1.0, 0.0), jnp.where(info[:, 1:2] + n_v == band, 1.0, 0.0)],
            axis=0,
        ).astype(BF16)
        for i in range(GRID):
            at = slice(i * plane, (i + 1) * plane)
            both = dot(hot, bands[:, at])
            dens = both[:CHUNK] * both[CHUNK:]
            high = dens.astype(BF16)
            span = slice(i * CHUNK, (i + 1) * CHUNK)
            dens_h[span, :] = high
            dens_l[span, :] = (dens - high.astype(F32)).astype(BF16)
        if first_chunk:
            loads[2].wait()
            loads[3].wait()
        middle = GRID // 2
        start = []
        for part in range(2):
            at = slice(part * width, (part + 1) * width)
            value = (
                dot(dens_h[...], first_h[:, at])
                + dot(dens_l[...], first_h[:, at])
                + dot(dens_h[...], first_l[:, at])
            ).reshape(GRID, CHUNK, width)
            start.append(value[0])
            for i in range(1, middle + 1):
                span = slice((i - 1) * CHUNK, i * CHUNK)
                even, odd = value[i], jnp.zeros((CHUNK, width), F32)
                if i < middle:
                    even, odd = value[i] + value[GRID - i], value[i] - value[GRID - i]
                for whole, top, rest in ((even, even_h, even_l), (odd, odd_h, odd_l)):
                    high = whole.astype(BF16)
                    top[span, at] = high
                    rest[span, at] = (whole - high.astype(F32)).astype(BF16)
        if first_chunk:
            loads[4].wait()
            loads[5].wait()
        both = []
        for which, top, rest in ((0, even_h, even_l), (1, odd_h, odd_l)):
            value = (
                dot(second_h[which], top[...])
                + dot(second_h[which], rest[...])
                + dot(second_l[which], top[...])
            )
            both.append(value.reshape(reach + 1, CHUNK, 2 * width))
        even, odd = both
        for a in range(reach + 1):
            even_r, even_i = even[a, :, :width] + start[0], even[a, :, width:] + start[1]
            odd_r, odd_i = odd[a, :, :width], odd[a, :, width:]
            parts = [(reach + a, even_r + odd_i, even_i - odd_r)]
            if a:
                parts.append((reach - a, even_r - odd_i, even_i + odd_r))
            for at, real, imag in parts:
                at = 2 * CHUNK * at
                spec[n, at:at + CHUNK, :] = (real * factor).astype(BF16)
                spec[n, at + CHUNK:at + 2 * CHUNK, :] = (imag * factor).astype(BF16)

    transform(0, True)
    if chunks > 1:
        @pl.loop(1, chunks)
        def _(n):
            transform(n, False)

    height = 2 * CHUNK
    low, high = (reach - short) * height, (reach + short + 1) * height

    def select(n, source, size, out, target):
        here = pl.ds(source, size)
        a, sign = facts[0, :, here], facts[1, :, here]
        a = jnp.concatenate([a] * (2 * CHUNK // SUBLANES), axis=0)
        sign = jnp.concatenate([sign] * (CHUNK // SUBLANES), axis=0)
        hot = hots.at[:, here]
        picked = dot(spec[n, :, :MAIN], hot[:MAIN, :])
        if width > MAIN:
            more = dot(spec[n, low:high, MAIN:keys.shape[0]], hot[MAIN:, :])
        total = jnp.zeros((height, size), F32)
        for k in range(2 * reach + 1):
            value = picked[k * height:(k + 1) * height]
            if width > MAIN and low <= k * height < high:
                value = value + more[k * height - low:(k + 1) * height - low]
            total = jnp.where(a == float(k - reach), value, total)
        imag = total[CHUNK:]
        at = pl.ds(target, size)
        out[n, :CHUNK, at] = total[:CHUNK].astype(BF16)
        out[n, CHUNK:, at] = (imag * sign).astype(BF16)

    def block(source, target, size, out):
        def run(n):
            for done in range(0, size, TILE):
                at = source + done
                at = at if isinstance(at, int) else pl.multiple_of(at, LANES)
                select(n, at, min(TILE, size - done), out, target + done)

        if chunks == 1:
            run(0)
        else:
            pl.loop(0, chunks)(run)

    piece = max(x for x in range(LANES, PIECE + 1, LANES) if col_pad % x == 0)
    parts = col_pad // piece

    def col_copy(step, part):
        peer = (chip + step) % n_chip * 2 + core
        here = cols.at[me, :, :, pl.ds(part * piece, piece)]
        return pltpu.make_async_remote_copy(
            src_ref=here, dst_ref=here,
            send_sem=col_send.at[step, part], recv_sem=col_recv.at[step, part],
            device_id=sibling if step == 0 else {"pair": peer}, device_id_type=MESH,
        )

    def relay_copy(step, part):
        source = (chip + n_chip - step) % n_chip * 2 + core
        here = cols.at[source, :, :, pl.ds(part * piece, piece)]
        return pltpu.make_async_remote_copy(
            src_ref=here, dst_ref=here,
            send_sem=relay_send.at[step, part], recv_sem=relay_recv.at[step, part],
            device_id=sibling, device_id_type=MESH,
        )

    def row_copy(step):
        return pltpu.make_async_remote_copy(
            src_ref=row_buf.at[step], dst_ref=rows.at[me],
            send_sem=row_send.at[step], recv_sem=row_recv.at[step],
            device_id={"pair": pair_at(step)}, device_id_type=MESH,
        )

    for part in range(parts):
        block(part * piece, part * piece, piece, cols.at[me])
        for step in (*range(1, n_chip), 0):
            col_copy(step, part).start()

    def row_step(step, carry):
        block(col_pad + step * row_pad, 0, row_pad, row_buf.at[step])

        @pl.when(step != own_step)
        def _():
            row_copy(step).start()
        return carry

    lax.fori_loop(0, own_step, row_step, 0)
    for part in range(parts):
        for step in range(1, n_chip):
            col_copy(step, part).wait_recv()
            relay_copy(step, part).start()
    lax.fori_loop(own_step, n_pair, row_step, 0)
    rows[me] = row_buf[own_step]

    for part in range(parts):
        for step in range(1, n_chip):
            col_copy(step, part).wait_send()
            relay_copy(step, part).wait()
        col_copy(0, part).wait()

    def row_wait(step, carry):
        @pl.when(step != own_step)
        def _():
            row_copy(step).wait()
        return carry

    lax.fori_loop(0, n_pair, row_wait, 0)


def panels(ids, energy_v, energy_c, g_list, valence, conduction, total_g, col_pad, row_pad, layout):
    reach, short, width, keys, first, second = tables(total_g)
    n_pair, n_grow, n_gcol, per_device, chunks = layout[:5]
    consts = [jnp.asarray(x) for x in (*first, *second)]
    large = [valence, conduction, *consts]
    args = [energy_v, energy_c, g_list, jnp.asarray(keys)]
    height = 2 * CHUNK * (2 * reach + 1)
    half = GRID * CHUNK
    n_group = n_grow * n_gcol
    n_v, n_c = valence.shape[0], conduction.shape[0]
    vmem = pl.BlockSpec(memory_space=pltpu.VMEM)
    dma = pltpu.SemaphoreType.DMA
    return pl.pallas_call(
        functools.partial(body, reach, short, width, layout),
        out_shape=[
            jax.ShapeDtypeStruct((n_pair, chunks, 2 * CHUNK, col_pad), BF16),
            jax.ShapeDtypeStruct((n_pair, chunks, 2 * CHUNK, row_pad), BF16),
        ],
        in_specs=[pl.BlockSpec(memory_space=pltpu.SMEM)] * len(ids) + [vmem] * len(args)
        + [pl.BlockSpec(memory_space=pl.ANY)] * len(large),
        out_specs=[vmem] * 2,
        scratch_shapes=[pltpu.VMEM((n_v + n_c, GRID**3), BF16)]
        + [pltpu.VMEM(x.shape, x.dtype) for x in consts] + [
            pltpu.VMEM((n_group + 1, CHUNK, LANES), jnp.int32),
            pltpu.VMEM((half, GRID * GRID), BF16),
            pltpu.VMEM((half, GRID * GRID), BF16),
            *[pltpu.VMEM((half // 2, 2 * width), BF16)] * 4,
            pltpu.VMEM((chunks, height, width), BF16),
            pltpu.VMEM((n_pair, chunks, 2 * CHUNK, row_pad), BF16),
            pltpu.VMEM((keys.shape[0], col_pad + n_pair * row_pad), BF16),
            pltpu.VMEM((2, SUBLANES, col_pad + n_pair * row_pad), F32),
            dma((len(large),)),
            dma((n_group,)), dma((n_group,)),
            *[dma((n_pair // 2, col_pad // LANES))] * 4,
            dma((n_pair,)), dma((n_pair,)),
        ],
        compiler_params=pltpu.CompilerParams(
            collective_id=0, has_side_effects=True, vmem_limit_bytes=56 * 2**20
        ),
    )(*ids, *args, *large)


def product_kernel(scale, pieces, rows, cols, out, turned, held, sem):
    turned[...] = rows[...].T
    step = out.shape[0] // pieces
    copies = []
    for n in range(pieces):
        at = pl.ds(n * step, step)
        held[at, :] = jnp.dot(turned[at, :], cols[...], preferred_element_type=F32) * scale
        copies.append(pltpu.make_async_copy(held.at[at], out.at[at], sem.at[n]))
        copies[-1].start()
    for copy in copies:
        copy.wait()


def product(rows, cols, n_rows, n_cols, scale):
    depth, row_pad = rows.shape
    pieces = max(x for x in range(1, 9) if n_rows % (16 * x) == 0)
    return pl.pallas_call(
        functools.partial(product_kernel, scale, pieces),
        out_shape=jax.ShapeDtypeStruct((n_rows, n_cols), F32),
        in_specs=[pl.BlockSpec(memory_space=pltpu.VMEM)] * 2,
        out_specs=pl.BlockSpec(memory_space=pl.ANY),
        scratch_shapes=[
            pltpu.VMEM((row_pad, depth), BF16),
            pltpu.VMEM((n_rows, n_cols), F32),
            pltpu.SemaphoreType.DMA((pieces,)),
        ],
        compiler_params=pltpu.CompilerParams(vmem_limit_bytes=62 * 2**20),
    )(rows, cols)


def local(
    valence,
    conduction,
    valence_energy,
    conduction_energy,
    pair_valence,
    pair_conduction,
    pair_count,
    g_index,
):
    slot_count = pair_valence.shape[0]
    total_g = g_index.shape[0]
    n_pair = lax.axis_size("pair")
    n_grow = lax.axis_size("grow")
    n_gcol = lax.axis_size("gcol")
    sub_rows = total_g // (n_pair * n_grow)
    col_width = total_g // n_gcol
    row_pad, col_pad = pad_to(sub_rows, LANES), pad_to(col_width, LANES)
    if row_pad == sub_rows and col_pad == col_width:
        g_list = g_index[None, :]
        col_at = lambda gcol: gcol * col_width
        row_at = lambda pair, grow: (pair * n_grow + grow) * sub_rows
    else:
        by_col = jnp.pad(g_index.reshape(n_gcol, col_width), ((0, 0), (0, col_pad - col_width)))
        by_row = jnp.pad(g_index.reshape(-1, sub_rows), ((0, 0), (0, row_pad - sub_rows)))
        g_list = jnp.concatenate([by_col.reshape(-1), by_row.reshape(-1)])[None, :]
        col_at = lambda gcol: gcol * col_pad
        row_at = lambda pair, grow: n_gcol * col_pad + (pair * n_grow + grow) * row_pad
    chunks = slot_count * n_grow * n_gcol // CHUNK
    layout = (n_pair, n_grow, n_gcol, slot_count, chunks, col_at, row_at)
    cols, rows = panels(
        (pair_valence, pair_conduction, pair_count), valence_energy[None, :], conduction_energy[None, :], g_list,
        valence, conduction, total_g, col_pad, row_pad, layout,
    )
    total_slots = slot_count * n_pair * n_grow * n_gcol
    return product(
        rows.reshape(-1, row_pad), cols.reshape(-1, col_pad), sub_rows, col_width,
        -1.0 / math.sqrt(total_slots),
    )


def solution(mesh):
    return jax.shard_map(
        local,
        mesh=mesh,
        in_specs=(
            P(),
            P("pair", None),
            P(),
            P("pair"),
            P(("pair", "grow", "gcol")),
            P(("pair", "grow", "gcol")),
            P(("pair", "grow", "gcol")),
            P(),
        ),
        out_specs=P(("pair", "grow"), "gcol"),
        check_vma=False,
    )
```

```python
import functools
import math

import jax
import jax.numpy as jnp
import ml_dtypes
import numpy as np
from jax import lax
from jax.experimental import pallas as pl
from jax.experimental.pallas import tpu as pltpu
from jax.sharding import PartitionSpec as P

GRID = 32
BITS = 5
CHUNK = 16
LANES = 128
SUBLANES = 8
TILE = 256
MAIN = 256
PIECE = 1152
MESH = pl.DeviceIdType.MESH
BF16 = jnp.bfloat16
F32 = jnp.float32


def pad_to(size, unit):
    return -(-size // unit) * unit


def ball(total_g):
    freq = np.arange(-(GRID // 2) + 1, GRID // 2)
    square = freq[:, None, None] ** 2 + freq[None, :, None] ** 2 + freq[None, None, :] ** 2
    return int(np.sort(square.ravel())[total_g])


def split(values):
    high = values.astype(ml_dtypes.bfloat16)
    low = (values - high.astype(np.float64)).astype(ml_dtypes.bfloat16)
    return high, low


def tables(total_g):
    limit = ball(total_g)
    reach = math.isqrt(limit)
    plane = []
    for b in range(0, reach + 1):
        for c in range(-reach, reach + 1):
            if b * b + c * c <= limit and (b > 0 or c >= 0):
                plane.append((b * b + c * c, b, c))
    plane.sort()
    extra = plane[MAIN:]
    short = math.isqrt(limit - extra[0][0]) if extra else -1
    width = pad_to(len(plane), LANES)
    keys = np.full((width,), -1, np.int32)
    bs = np.zeros((width,), np.int64)
    cs = np.zeros((width,), np.int64)
    for at, (_, b, c) in enumerate(plane):
        keys[at] = b * GRID + c + GRID // 2
        bs[at], cs[at] = b, c
    cell = np.arange(GRID * GRID)
    phase = (cell[:, None] // GRID * bs[None] + cell[:, None] % GRID * cs[None]) % GRID
    angle = phase * (2.0 * math.pi / GRID)
    used = keys[None] >= 0
    first = np.concatenate([np.cos(angle) * used, -np.sin(angle) * used], axis=1)
    points = np.arange(1, GRID // 2 + 1)
    angle = (np.arange(reach + 1)[:, None] * points[None] % GRID) * (2.0 * math.pi / GRID)
    second = np.stack([np.cos(angle), np.sin(angle)])
    second = np.kron(second, np.eye(CHUNK)[None])
    keys = np.repeat(keys[: pad_to(len(plane), CHUNK), None], TILE, axis=1)
    return reach, short, width, keys, split(first), split(second)


def body(
    reach, short, width, layout,
    ids_v, ids_c, count, energy_v, energy_c, g_list, keys, valence_in, conduction_in, *refs,
):
    n_pair, n_grow, n_gcol, per_device, chunks, col_at, row_at = layout
    tables_in, (cols, rows), scratch = refs[:4], refs[4:6], refs[6:]
    bands, first_h, first_l, second_h, second_l = scratch[:5]
    infos, dens_h, dens_l, even_h, even_l, odd_h, odd_l, spec, row_buf, hots, facts = scratch[5:16]
    tile_info = infos.at[n_grow * n_gcol]
    load_sem, info_send, info_recv, col_send, col_recv, relay_send, relay_recv, row_send, row_recv = scratch[16:]
    n_v, n_c = valence_in.shape[0], conduction_in.shape[0]

    me, grow, gcol = lax.axis_index("pair"), lax.axis_index("grow"), lax.axis_index("gcol")
    chip, core = me // 2, me % 2
    n_chip, n_group = n_pair // 2, n_grow * n_gcol
    group = grow * n_gcol + gcol
    sibling = {"pair": chip * 2 + (1 - core)}

    def group_id(step):
        other = (group + step) % n_group
        return {"grow": other // n_gcol, "gcol": other % n_gcol}

    def pair_at(step):
        return (chip + 1 + step // 2) % n_chip * 2 + (core + step % 2) % 2

    own_step = (n_chip - 1) * 2

    loads = [
        pltpu.make_async_copy(source, target, load_sem.at[n])
        for n, (source, target) in enumerate(
            zip(
                (valence_in, conduction_in, *tables_in),
                (bands.at[pl.ds(0, n_v)], bands.at[pl.ds(n_v, n_c)], *scratch[1:5]),
            )
        )
    ]
    for load in loads:
        load.start()

    slot = lax.broadcasted_iota(jnp.int32, (CHUNK, LANES), 0) % per_device
    lane = lax.broadcasted_iota(jnp.int32, (CHUNK, LANES), 1)
    mine = jnp.zeros((CHUNK, LANES), jnp.int32)
    for j in range(per_device):
        live = jnp.where(count[0] > j, 1, 0)
        row = jnp.where(lane == 0, ids_v[j], jnp.where(lane == 1, ids_c[j], live))
        mine = jnp.where(slot == j, row, mine)
    tile_info[...] = mine

    def facts_of(source, size):
        cell = g_list[:, pl.ds(source, size)]
        cell = jnp.broadcast_to(cell, (SUBLANES, size))
        centre = lambda v: jnp.where(v < GRID // 2, v, v - GRID)
        a = centre(cell >> (2 * BITS))
        b = centre((cell >> BITS) & (GRID - 1))
        c = centre(cell & (GRID - 1))
        flip = (b < 0) | ((b == 0) & (c < 0))
        a = jnp.where(flip, -a, a)
        b = jnp.where(flip, -b, b)
        c = jnp.where(flip, -c, c)
        key = b * GRID + c + GRID // 2
        key = jnp.concatenate([key] * (CHUNK // SUBLANES), axis=0)
        hot = [
            jnp.where(keys[at:at + CHUNK, :size] == key, 1.0, 0.0).astype(BF16)
            for at in range(0, keys.shape[0], CHUNK)
        ]
        return a.astype(F32), jnp.where(flip, -1.0, 1.0), hot

    def prepare(source, target, size):
        here = pl.ds(target, size)
        facts[0, :, here], facts[1, :, here], hot = facts_of(source, size)
        for n, rows_of in enumerate(hot):
            hots[n * CHUNK:(n + 1) * CHUNK, here] = rows_of

    def prepare_block(source, target, size):
        @pl.loop(0, size // LANES)
        def _(t):
            prepare(
                pl.multiple_of(source + t * LANES, LANES),
                pl.multiple_of(target + t * LANES, LANES), LANES,
            )

    col_pad, row_pad = cols.shape[-1], rows.shape[-1]
    barrier = pltpu.get_barrier_semaphore()

    def greet_group(step, carry):
        pl.semaphore_signal(barrier, inc=1, device_id=group_id(step), device_id_type=MESH)
        return carry

    def greet_pair(step, carry):
        @pl.when(step != own_step)
        def _():
            pl.semaphore_signal(
                barrier, inc=1, device_id={"pair": pair_at(step)}, device_id_type=MESH
            )
        return carry

    lax.fori_loop(1, n_group, greet_group, 0)
    lax.fori_loop(0, n_pair, greet_pair, 0)
    prepare_block(col_at(gcol), 0, col_pad)
    pl.semaphore_wait(barrier, n_group - 1 + n_pair - 1)

    def info_copy(step):
        return pltpu.make_async_remote_copy(
            src_ref=tile_info, dst_ref=infos.at[group],
            send_sem=info_send.at[step], recv_sem=info_recv.at[step],
            device_id=group_id(step), device_id_type=MESH,
        )

    def start_info(step, carry):
        info_copy(step).start()
        return carry

    def wait_info(step, carry):
        info_copy(step).wait()
        return carry

    lax.fori_loop(1, n_group, start_info, 0)
    infos[group] = mine

    prepare_block(row_at(pair_at(0), grow), col_pad, row_pad)

    lax.fori_loop(1, n_group, wait_info, 0)

    plane = GRID * GRID
    together = CHUNK // per_device
    dot = functools.partial(jnp.dot, preferred_element_type=F32)
    loads[0].wait()
    loads[1].wait()

    def transform(n, first_chunk):
        slot = lax.broadcasted_iota(jnp.int32, (CHUNK, LANES), 0)
        info = jnp.zeros((CHUNK, LANES), jnp.int32)
        for d in range(together):
            info = jnp.where(slot // per_device == d, infos[n * together + d], info)
        pick_v = info[:, 0:1] == lax.broadcasted_iota(jnp.int32, (CHUNK, n_v), 1)
        pick_c = info[:, 1:2] == lax.broadcasted_iota(jnp.int32, (CHUNK, n_c), 1)
        live = info[:, 2:3].astype(F32)
        gap = jnp.sum(jnp.where(pick_c, energy_c[...], 0.0), axis=1, keepdims=True) - jnp.sum(
            jnp.where(pick_v, energy_v[...], 0.0), axis=1, keepdims=True
        )
        factor = live * jnp.sqrt(4.0 / gap) / math.sqrt(GRID**3)
        band = lax.broadcasted_iota(jnp.int32, (CHUNK, n_v + n_c), 1)
        hot = jnp.concatenate(
            [jnp.where(info[:, 0:1] == band, 1.0, 0.0), jnp.where(info[:, 1:2] + n_v == band, 1.0, 0.0)],
            axis=0,
        ).astype(BF16)
        for i in range(GRID):
            at = slice(i * plane, (i + 1) * plane)
            both = dot(hot, bands[:, at])
            dens = both[:CHUNK] * both[CHUNK:]
            high = dens.astype(BF16)
            span = slice(i * CHUNK, (i + 1) * CHUNK)
            dens_h[span, :] = high
            dens_l[span, :] = (dens - high.astype(F32)).astype(BF16)
        if first_chunk:
            loads[2].wait()
            loads[3].wait()
        middle = GRID // 2
        start = []
        for part in range(2):
            at = slice(part * width, (part + 1) * width)
            value = (
                dot(dens_h[...], first_h[:, at])
                + dot(dens_l[...], first_h[:, at])
                + dot(dens_h[...], first_l[:, at])
            ).reshape(GRID, CHUNK, width)
            start.append(value[0])
            for i in range(1, middle + 1):
                span = slice((i - 1) * CHUNK, i * CHUNK)
                even, odd = value[i], jnp.zeros((CHUNK, width), F32)
                if i < middle:
                    even, odd = value[i] + value[GRID - i], value[i] - value[GRID - i]
                for whole, top, rest in ((even, even_h, even_l), (odd, odd_h, odd_l)):
                    high = whole.astype(BF16)
                    top[span, at] = high
                    rest[span, at] = (whole - high.astype(F32)).astype(BF16)
        if first_chunk:
            loads[4].wait()
            loads[5].wait()
        both = []
        for which, top, rest in ((0, even_h, even_l), (1, odd_h, odd_l)):
            value = (
                dot(second_h[which], top[...])
                + dot(second_h[which], rest[...])
                + dot(second_l[which], top[...])
            )
            both.append(value.reshape(reach + 1, CHUNK, 2 * width))
        even, odd = both
        for a in range(reach + 1):
            even_r, even_i = even[a, :, :width] + start[0], even[a, :, width:] + start[1]
            odd_r, odd_i = odd[a, :, :width], odd[a, :, width:]
            parts = [(reach + a, even_r + odd_i, even_i - odd_r)]
            if a:
                parts.append((reach - a, even_r - odd_i, even_i + odd_r))
            for at, real, imag in parts:
                at = 2 * CHUNK * at
                spec[n, at:at + CHUNK, :] = (real * factor).astype(BF16)
                spec[n, at + CHUNK:at + 2 * CHUNK, :] = (imag * factor).astype(BF16)

    transform(0, True)
    if chunks > 1:
        @pl.loop(1, chunks)
        def _(n):
            transform(n, False)

    height = 2 * CHUNK
    low, high = (reach - short) * height, (reach + short + 1) * height

    def select(n, source, size, out, target, ready):
        here = pl.ds(source, size)
        if ready:
            a, sign = facts[0, :, here], facts[1, :, here]
            hot = [hots[:MAIN, here], hots[MAIN:, here]]
        else:
            a, sign, hot = facts_of(source, size)
            cut = MAIN // CHUNK
            hot = [jnp.concatenate(hot[:cut], axis=0)] + [
                jnp.concatenate(hot[cut:], axis=0) for _ in range(1) if width > MAIN
            ]
        a = jnp.concatenate([a] * (2 * CHUNK // SUBLANES), axis=0)
        sign = jnp.concatenate([sign] * (CHUNK // SUBLANES), axis=0)
        picked = dot(spec[n, :, :MAIN], hot[0])
        if width > MAIN:
            more = dot(spec[n, low:high, MAIN:keys.shape[0]], hot[1])
        total = jnp.zeros((height, size), F32)
        for k in range(2 * reach + 1):
            value = picked[k * height:(k + 1) * height]
            if width > MAIN and low <= k * height < high:
                value = value + more[k * height - low:(k + 1) * height - low]
            total = jnp.where(a == float(k - reach), value, total)
        imag = total[CHUNK:]
        at = pl.ds(target, size)
        out[n, :CHUNK, at] = total[:CHUNK].astype(BF16)
        out[n, CHUNK:, at] = (imag * sign).astype(BF16)

    def block(source, size, out, target, ready):
        def run(n):
            for done in range(0, size, TILE):
                at = source + done
                at = at if isinstance(at, int) else pl.multiple_of(at, LANES)
                select(n, at, min(TILE, size - done), out, target + done, ready)

        if chunks == 1:
            run(0)
        else:
            pl.loop(0, chunks)(run)

    piece = max(x for x in range(LANES, PIECE + 1, LANES) if col_pad % x == 0)
    parts = col_pad // piece

    def col_copy(step, part):
        peer = (chip + step) % n_chip * 2 + core
        here = cols.at[me, :, :, pl.ds(part * piece, piece)]
        return pltpu.make_async_remote_copy(
            src_ref=here, dst_ref=here,
            send_sem=col_send.at[step, part], recv_sem=col_recv.at[step, part],
            device_id=sibling if step == 0 else {"pair": peer}, device_id_type=MESH,
        )

    def relay_copy(step, part):
        source = (chip + n_chip - step) % n_chip * 2 + core
        here = cols.at[source, :, :, pl.ds(part * piece, piece)]
        return pltpu.make_async_remote_copy(
            src_ref=here, dst_ref=here,
            send_sem=relay_send.at[step, part], recv_sem=relay_recv.at[step, part],
            device_id=sibling, device_id_type=MESH,
        )

    def row_copy(step):
        return pltpu.make_async_remote_copy(
            src_ref=row_buf.at[step], dst_ref=rows.at[me],
            send_sem=row_send.at[step], recv_sem=row_recv.at[step],
            device_id={"pair": pair_at(step)}, device_id_type=MESH,
        )

    for part in range(parts):
        block(part * piece, piece, cols.at[me], part * piece, True)
        for step in (*range(1, n_chip), 0):
            col_copy(step, part).start()

    def row_step(step, carry):
        first = isinstance(step, int)
        source = col_pad if first else row_at(pair_at(step), grow)
        block(source, row_pad, row_buf.at[step], 0, first)

        @pl.when(step != own_step)
        def _():
            row_copy(step).start()
        return carry

    row_step(0, 0)
    lax.fori_loop(1, own_step, row_step, 0)
    for part in range(parts):
        for step in range(1, n_chip):
            col_copy(step, part).wait_recv()
            relay_copy(step, part).start()
    lax.fori_loop(own_step, n_pair, row_step, 0)
    rows[me] = row_buf[own_step]

    for part in range(parts):
        for step in range(1, n_chip):
            col_copy(step, part).wait_send()
            relay_copy(step, part).wait()
        col_copy(0, part).wait()

    def row_wait(step, carry):
        @pl.when(step != own_step)
        def _():
            row_copy(step).wait()
        return carry

    lax.fori_loop(0, n_pair, row_wait, 0)


def panels(ids, energy_v, energy_c, g_list, valence, conduction, total_g, col_pad, row_pad, layout):
    reach, short, width, keys, first, second = tables(total_g)
    n_pair, n_grow, n_gcol, per_device, chunks = layout[:5]
    consts = [jnp.asarray(x) for x in (*first, *second)]
    large = [valence, conduction, *consts]
    args = [energy_v, energy_c, g_list, jnp.asarray(keys)]
    height = 2 * CHUNK * (2 * reach + 1)
    half = GRID * CHUNK
    n_group = n_grow * n_gcol
    n_v, n_c = valence.shape[0], conduction.shape[0]
    vmem = pl.BlockSpec(memory_space=pltpu.VMEM)
    dma = pltpu.SemaphoreType.DMA
    return pl.pallas_call(
        functools.partial(body, reach, short, width, layout),
        out_shape=[
            jax.ShapeDtypeStruct((n_pair, chunks, 2 * CHUNK, col_pad), BF16),
            jax.ShapeDtypeStruct((n_pair, chunks, 2 * CHUNK, row_pad), BF16),
        ],
        in_specs=[pl.BlockSpec(memory_space=pltpu.SMEM)] * len(ids) + [vmem] * len(args)
        + [pl.BlockSpec(memory_space=pl.ANY)] * len(large),
        out_specs=[vmem] * 2,
        scratch_shapes=[pltpu.VMEM((n_v + n_c, GRID**3), BF16)]
        + [pltpu.VMEM(x.shape, x.dtype) for x in consts] + [
            pltpu.VMEM((n_group + 1, CHUNK, LANES), jnp.int32),
            pltpu.VMEM((half, GRID * GRID), BF16),
            pltpu.VMEM((half, GRID * GRID), BF16),
            *[pltpu.VMEM((half // 2, 2 * width), BF16)] * 4,
            pltpu.VMEM((chunks, height, width), BF16),
            pltpu.VMEM((n_pair, chunks, 2 * CHUNK, row_pad), BF16),
            pltpu.VMEM((keys.shape[0], col_pad + row_pad), BF16),
            pltpu.VMEM((2, SUBLANES, col_pad + row_pad), F32),
            dma((len(large),)),
            dma((n_group,)), dma((n_group,)),
            *[dma((n_pair // 2, col_pad // LANES))] * 4,
            dma((n_pair,)), dma((n_pair,)),
        ],
        compiler_params=pltpu.CompilerParams(
            collective_id=0, has_side_effects=True, vmem_limit_bytes=56 * 2**20
        ),
    )(*ids, *args, *large)


def product_kernel(scale, pieces, rows, cols, out, turned, held, sem):
    turned[...] = rows[...].T
    copies = []
    for n, (start, step) in enumerate(pieces):
        at = pl.ds(start, step)
        held[at, :] = jnp.dot(turned[at, :], cols[...], preferred_element_type=F32) * scale
        copies.append(pltpu.make_async_copy(held.at[at], out.at[at], sem.at[n]))
        copies[-1].start()
    for copy in copies:
        copy.wait()


def product(rows, cols, n_rows, n_cols, scale):
    depth, row_pad = rows.shape
    pieces, start = [], 0
    while start < n_rows:
        step = min(CHUNK * (1 << min(len(pieces) + 1, 3)), n_rows - start)
        pieces.append((start, step))
        start += step
    return pl.pallas_call(
        functools.partial(product_kernel, scale, pieces),
        out_shape=jax.ShapeDtypeStruct((n_rows, n_cols), F32),
        in_specs=[pl.BlockSpec(memory_space=pltpu.VMEM)] * 2,
        out_specs=pl.BlockSpec(memory_space=pl.ANY),
        scratch_shapes=[
            pltpu.VMEM((row_pad, depth), BF16),
            pltpu.VMEM((n_rows, n_cols), F32),
            pltpu.SemaphoreType.DMA((len(pieces),)),
        ],
        compiler_params=pltpu.CompilerParams(vmem_limit_bytes=62 * 2**20),
    )(rows, cols)


def local(
    valence,
    conduction,
    valence_energy,
    conduction_energy,
    pair_valence,
    pair_conduction,
    pair_count,
    g_index,
):
    slot_count = pair_valence.shape[0]
    total_g = g_index.shape[0]
    n_pair = lax.axis_size("pair")
    n_grow = lax.axis_size("grow")
    n_gcol = lax.axis_size("gcol")
    sub_rows = total_g // (n_pair * n_grow)
    col_width = total_g // n_gcol
    row_pad, col_pad = pad_to(sub_rows, LANES), pad_to(col_width, LANES)
    if row_pad == sub_rows and col_pad == col_width:
        g_list = g_index[None, :]
        col_at = lambda gcol: gcol * col_width
        row_at = lambda pair, grow: (pair * n_grow + grow) * sub_rows
    else:
        by_col = jnp.pad(g_index.reshape(n_gcol, col_width), ((0, 0), (0, col_pad - col_width)))
        by_row = jnp.pad(g_index.reshape(-1, sub_rows), ((0, 0), (0, row_pad - sub_rows)))
        g_list = jnp.concatenate([by_col.reshape(-1), by_row.reshape(-1)])[None, :]
        col_at = lambda gcol: gcol * col_pad
        row_at = lambda pair, grow: n_gcol * col_pad + (pair * n_grow + grow) * row_pad
    chunks = slot_count * n_grow * n_gcol // CHUNK
    layout = (n_pair, n_grow, n_gcol, slot_count, chunks, col_at, row_at)
    cols, rows = panels(
        (pair_valence, pair_conduction, pair_count), valence_energy[None, :], conduction_energy[None, :], g_list,
        valence, conduction, total_g, col_pad, row_pad, layout,
    )
    total_slots = slot_count * n_pair * n_grow * n_gcol
    return product(
        rows.reshape(-1, row_pad), cols.reshape(-1, col_pad), sub_rows, col_width,
        -1.0 / math.sqrt(total_slots),
    )


def solution(mesh):
    return jax.shard_map(
        local,
        mesh=mesh,
        in_specs=(
            P(),
            P("pair", None),
            P(),
            P("pair"),
            P(("pair", "grow", "gcol")),
            P(("pair", "grow", "gcol")),
            P(("pair", "grow", "gcol")),
            P(),
        ),
        out_specs=P(("pair", "grow"), "gcol"),
        check_vma=False,
    )
```

```python
import functools
import math

import jax
import jax.numpy as jnp
import ml_dtypes
import numpy as np
from jax import lax
from jax.experimental import pallas as pl
from jax.experimental.pallas import tpu as pltpu
from jax.sharding import PartitionSpec as P

GRID = 32
BITS = 5
CHUNK = 16
LANES = 128
TILE = 256
MAIN = 256
PIECE = 1152
MESH = pl.DeviceIdType.MESH
BF16 = jnp.bfloat16
F32 = jnp.float32


def pad_to(size, unit):
    return -(-size // unit) * unit


def ball(total_g):
    freq = np.arange(-(GRID // 2) + 1, GRID // 2)
    square = freq[:, None, None] ** 2 + freq[None, :, None] ** 2 + freq[None, None, :] ** 2
    return int(np.sort(square.ravel())[total_g])


def split(values):
    high = values.astype(ml_dtypes.bfloat16)
    low = (values - high.astype(np.float64)).astype(ml_dtypes.bfloat16)
    return high, low


def tables(total_g):
    limit = ball(total_g)
    reach = math.isqrt(limit)
    plane = []
    for b in range(0, reach + 1):
        for c in range(-reach, reach + 1):
            if b * b + c * c <= limit and (b > 0 or c >= 0):
                plane.append((b * b + c * c, b, c))
    plane.sort()
    extra = plane[MAIN:]
    short = math.isqrt(limit - extra[0][0]) if extra else -1
    width = pad_to(len(plane), LANES)
    keys = np.full((width,), -1, np.int32)
    bs = np.zeros((width,), np.int64)
    cs = np.zeros((width,), np.int64)
    for at, (_, b, c) in enumerate(plane):
        keys[at] = b * GRID + c + GRID // 2
        bs[at], cs[at] = b, c
    cell = np.arange(GRID * GRID)
    phase = (cell[:, None] // GRID * bs[None] + cell[:, None] % GRID * cs[None]) % GRID
    angle = phase * (2.0 * math.pi / GRID)
    used = keys[None] >= 0
    first = np.concatenate([np.cos(angle) * used, -np.sin(angle) * used], axis=1)
    points = np.arange(1, GRID // 2 + 1)
    angle = (np.arange(reach + 1)[:, None] * points[None] % GRID) * (2.0 * math.pi / GRID)
    second = np.stack([np.cos(angle), np.sin(angle)])
    second = np.kron(second, np.eye(CHUNK)[None])
    keys = np.repeat(keys[: pad_to(len(plane), CHUNK), None], TILE, axis=1)
    return reach, short, width, keys, split(first), split(second)


def body(
    reach, short, width, layout,
    ids_v, ids_c, count, energy_v, energy_c, g_list, keys, valence_in, conduction_in, *refs,
):
    n_pair, n_grow, n_gcol, per_device, chunks, col_at, row_at = layout
    tables_in, (cols, rows), scratch = refs[:4], refs[4:6], refs[6:]
    bands, first_h, first_l, second_h, second_l = scratch[:5]
    infos, dens_h, dens_l, even_h, even_l, odd_h, odd_l, spec, row_buf = scratch[5:14]
    tile_info = infos.at[n_grow * n_gcol]
    load_sem, info_send, info_recv, col_send, col_recv, relay_send, relay_recv, row_send, row_recv = scratch[14:]
    n_v, n_c = valence_in.shape[0], conduction_in.shape[0]

    me, grow, gcol = lax.axis_index("pair"), lax.axis_index("grow"), lax.axis_index("gcol")
    chip, core = me // 2, me % 2
    n_chip, n_group = n_pair // 2, n_grow * n_gcol
    group = grow * n_gcol + gcol
    sibling = {"pair": chip * 2 + (1 - core)}

    def group_id(step):
        other = (group + step) % n_group
        return {"grow": other // n_gcol, "gcol": other % n_gcol}

    def pair_at(step):
        return (chip + 1 + step // 2) % n_chip * 2 + (core + step % 2) % 2

    own_step = (n_chip - 1) * 2

    loads = [
        pltpu.make_async_copy(source, target, load_sem.at[n])
        for n, (source, target) in enumerate(
            zip(
                (valence_in, conduction_in, *tables_in),
                (bands.at[pl.ds(0, n_v)], bands.at[pl.ds(n_v, n_c)], *scratch[1:5]),
            )
        )
    ]
    for load in loads:
        load.start()

    slot = lax.broadcasted_iota(jnp.int32, (CHUNK, LANES), 0) % per_device
    lane = lax.broadcasted_iota(jnp.int32, (CHUNK, LANES), 1)
    mine = jnp.zeros((CHUNK, LANES), jnp.int32)
    for j in range(per_device):
        live = jnp.where(count[0] > j, 1, 0)
        row = jnp.where(lane == 0, ids_v[j], jnp.where(lane == 1, ids_c[j], live))
        mine = jnp.where(slot == j, row, mine)
    tile_info[...] = mine

    barrier = pltpu.get_barrier_semaphore()

    def greet_group(step, carry):
        pl.semaphore_signal(barrier, inc=1, device_id=group_id(step), device_id_type=MESH)
        return carry

    def greet_pair(step, carry):
        @pl.when(step != own_step)
        def _():
            pl.semaphore_signal(
                barrier, inc=1, device_id={"pair": pair_at(step)}, device_id_type=MESH
            )
        return carry

    lax.fori_loop(1, n_group, greet_group, 0)
    lax.fori_loop(0, n_pair, greet_pair, 0)
    pl.semaphore_wait(barrier, n_group - 1 + n_pair - 1)

    def info_copy(step):
        return pltpu.make_async_remote_copy(
            src_ref=tile_info, dst_ref=infos.at[group],
            send_sem=info_send.at[step], recv_sem=info_recv.at[step],
            device_id=group_id(step), device_id_type=MESH,
        )

    def start_info(step, carry):
        info_copy(step).start()
        return carry

    def wait_info(step, carry):
        info_copy(step).wait()
        return carry

    lax.fori_loop(1, n_group, start_info, 0)
    infos[group] = mine
    lax.fori_loop(1, n_group, wait_info, 0)

    plane = GRID * GRID
    together = CHUNK // per_device
    dot = functools.partial(jnp.dot, preferred_element_type=F32)
    loads[0].wait()
    loads[1].wait()

    def transform(n, first_chunk):
        slot = lax.broadcasted_iota(jnp.int32, (CHUNK, LANES), 0)
        info = jnp.zeros((CHUNK, LANES), jnp.int32)
        for d in range(together):
            info = jnp.where(slot // per_device == d, infos[n * together + d], info)
        pick_v = info[:, 0:1] == lax.broadcasted_iota(jnp.int32, (CHUNK, n_v), 1)
        pick_c = info[:, 1:2] == lax.broadcasted_iota(jnp.int32, (CHUNK, n_c), 1)
        live = info[:, 2:3].astype(F32)
        gap = jnp.sum(jnp.where(pick_c, energy_c[...], 0.0), axis=1, keepdims=True) - jnp.sum(
            jnp.where(pick_v, energy_v[...], 0.0), axis=1, keepdims=True
        )
        factor = live * jnp.sqrt(4.0 / gap) / math.sqrt(GRID**3)
        band = lax.broadcasted_iota(jnp.int32, (CHUNK, n_v + n_c), 1)
        hot = jnp.concatenate(
            [jnp.where(info[:, 0:1] == band, 1.0, 0.0), jnp.where(info[:, 1:2] + n_v == band, 1.0, 0.0)],
            axis=0,
        ).astype(BF16)
        for i in range(GRID):
            at = slice(i * plane, (i + 1) * plane)
            both = dot(hot, bands[:, at])
            dens = both[:CHUNK] * both[CHUNK:]
            high = dens.astype(BF16)
            span = slice(i * CHUNK, (i + 1) * CHUNK)
            dens_h[span, :] = high
            dens_l[span, :] = (dens - high.astype(F32)).astype(BF16)
        if first_chunk:
            loads[2].wait()
            loads[3].wait()
        middle = GRID // 2
        start = []
        for part in range(2):
            at = slice(part * width, (part + 1) * width)
            value = (
                dot(dens_h[...], first_h[:, at])
                + dot(dens_l[...], first_h[:, at])
                + dot(dens_h[...], first_l[:, at])
            ).reshape(GRID, CHUNK, width)
            start.append(value[0])
            for i in range(1, middle + 1):
                span = slice((i - 1) * CHUNK, i * CHUNK)
                even, odd = value[i], jnp.zeros((CHUNK, width), F32)
                if i < middle:
                    even, odd = value[i] + value[GRID - i], value[i] - value[GRID - i]
                for whole, top, rest in ((even, even_h, even_l), (odd, odd_h, odd_l)):
                    high = whole.astype(BF16)
                    top[span, at] = high
                    rest[span, at] = (whole - high.astype(F32)).astype(BF16)
        if first_chunk:
            loads[4].wait()
            loads[5].wait()
        both = []
        for which, top, rest in ((0, even_h, even_l), (1, odd_h, odd_l)):
            value = (
                dot(second_h[which], top[...])
                + dot(second_h[which], rest[...])
                + dot(second_l[which], top[...])
            )
            both.append(value.reshape(reach + 1, CHUNK, 2 * width))
        even, odd = both
        for a in range(reach + 1):
            even_r, even_i = even[a, :, :width] + start[0], even[a, :, width:] + start[1]
            odd_r, odd_i = odd[a, :, :width], odd[a, :, width:]
            parts = [(reach + a, even_r + odd_i, even_i - odd_r)]
            if a:
                parts.append((reach - a, even_r - odd_i, even_i + odd_r))
            for at, real, imag in parts:
                at = 2 * CHUNK * at
                spec[n, at:at + CHUNK, :] = (real * factor).astype(BF16)
                spec[n, at + CHUNK:at + 2 * CHUNK, :] = (imag * factor).astype(BF16)

    transform(0, True)
    if chunks > 1:
        @pl.loop(1, chunks)
        def _(n):
            transform(n, False)

    height = 2 * CHUNK
    low, high = (reach - short) * height, (reach + short + 1) * height

    def select(n, source, size, out, target):
        cell = g_list[:, pl.ds(pl.multiple_of(source, LANES), size)]
        centre = lambda v: jnp.where(v < GRID // 2, v, v - GRID)
        a = centre(cell >> (2 * BITS))
        b = centre((cell >> BITS) & (GRID - 1))
        c = centre(cell & (GRID - 1))
        flip = (b < 0) | ((b == 0) & (c < 0))
        a = jnp.where(flip, -a, a)
        b = jnp.where(flip, -b, b)
        c = jnp.where(flip, -c, c)
        key = b * GRID + c + GRID // 2
        hot = jnp.where(keys[:, :size] == key, 1.0, 0.0).astype(BF16)
        picked = dot(spec[n, :, :MAIN], hot[:MAIN])
        if width > MAIN:
            more = dot(spec[n, low:high, MAIN:keys.shape[0]], hot[MAIN:])
        total = jnp.zeros((height, size), F32)
        for k in range(2 * reach + 1):
            value = picked[k * height:(k + 1) * height]
            if width > MAIN and low <= k * height < high:
                value = value + more[k * height - low:(k + 1) * height - low]
            total = jnp.where(a == k - reach, value, total)
        imag = total[CHUNK:]
        at = pl.ds(target, size)
        out[n, :CHUNK, at] = total[:CHUNK].astype(BF16)
        out[n, CHUNK:, at] = jnp.where(flip, -imag, imag).astype(BF16)

    def block(source, size, out):
        piece = max(x for x in range(LANES, PIECE + 1, LANES) if size % x == 0)

        def run(n):
            def part(t):
                for done in range(0, piece, TILE):
                    at = t * piece + done
                    at = at if isinstance(at, int) else pl.multiple_of(at, LANES)
                    select(n, source + at, min(TILE, piece - done), out, at)

            if size == piece:
                part(0)
            else:
                pl.loop(0, size // piece)(part)

        if chunks == 1:
            run(0)
        else:
            pl.loop(0, chunks)(run)

    def col_copy(step):
        peer = (chip + step) % n_chip * 2 + core
        return pltpu.make_async_remote_copy(
            src_ref=cols.at[me], dst_ref=cols.at[me],
            send_sem=col_send.at[step], recv_sem=col_recv.at[step],
            device_id=sibling if step == 0 else {"pair": peer}, device_id_type=MESH,
        )

    def relay_copy(step):
        source = (chip + n_chip - step) % n_chip * 2 + core
        return pltpu.make_async_remote_copy(
            src_ref=cols.at[source], dst_ref=cols.at[source],
            send_sem=relay_send.at[step], recv_sem=relay_recv.at[step],
            device_id=sibling, device_id_type=MESH,
        )

    def row_copy(step):
        return pltpu.make_async_remote_copy(
            src_ref=row_buf.at[step], dst_ref=rows.at[me],
            send_sem=row_send.at[step], recv_sem=row_recv.at[step],
            device_id={"pair": pair_at(step)}, device_id_type=MESH,
        )

    block(col_at(gcol), cols.shape[-1], cols.at[me])
    for step in (*range(1, n_chip), 0):
        col_copy(step).start()

    def row_step(step, carry):
        block(row_at(pair_at(step), grow), rows.shape[-1], row_buf.at[step])

        @pl.when(step != own_step)
        def _():
            row_copy(step).start()
        return carry

    lax.fori_loop(0, own_step, row_step, 0)
    for step in range(1, n_chip):
        col_copy(step).wait_recv()
        relay_copy(step).start()
    lax.fori_loop(own_step, n_pair, row_step, 0)
    rows[me] = row_buf[own_step]

    for step in range(1, n_chip):
        col_copy(step).wait_send()
        relay_copy(step).wait()
    col_copy(0).wait()

    def row_wait(step, carry):
        @pl.when(step != own_step)
        def _():
            row_copy(step).wait()
        return carry

    lax.fori_loop(0, n_pair, row_wait, 0)


def panels(ids, energy_v, energy_c, g_list, valence, conduction, total_g, col_pad, row_pad, layout):
    reach, short, width, keys, first, second = tables(total_g)
    n_pair, n_grow, n_gcol, per_device, chunks = layout[:5]
    consts = [jnp.asarray(x) for x in (*first, *second)]
    large = [valence, conduction, *consts]
    args = [energy_v, energy_c, g_list, jnp.asarray(keys)]
    height = 2 * CHUNK * (2 * reach + 1)
    half = GRID * CHUNK
    n_group = n_grow * n_gcol
    n_v, n_c = valence.shape[0], conduction.shape[0]
    vmem = pl.BlockSpec(memory_space=pltpu.VMEM)
    dma = pltpu.SemaphoreType.DMA
    return pl.pallas_call(
        functools.partial(body, reach, short, width, layout),
        out_shape=[
            pltpu.VMEM((n_pair, chunks, 2 * CHUNK, col_pad), BF16),
            pltpu.VMEM((n_pair, chunks, 2 * CHUNK, row_pad), BF16),
        ],
        in_specs=[pl.BlockSpec(memory_space=pltpu.SMEM)] * len(ids) + [vmem] * len(args)
        + [pl.BlockSpec(memory_space=pl.ANY)] * len(large),
        out_specs=[vmem] * 2,
        scratch_shapes=[pltpu.VMEM((n_v + n_c, GRID**3), BF16)]
        + [pltpu.VMEM(x.shape, x.dtype) for x in consts] + [
            pltpu.VMEM((n_group + 1, CHUNK, LANES), jnp.int32),
            pltpu.VMEM((half, GRID * GRID), BF16),
            pltpu.VMEM((half, GRID * GRID), BF16),
            *[pltpu.VMEM((half // 2, 2 * width), BF16)] * 4,
            pltpu.VMEM((chunks, height, width), BF16),
            pltpu.VMEM((n_pair, chunks, 2 * CHUNK, row_pad), BF16),
            dma((len(large),)),
            dma((n_group,)), dma((n_group,)),
            dma((n_pair // 2,)), dma((n_pair // 2,)),
            dma((n_pair // 2,)), dma((n_pair // 2,)),
            dma((n_pair,)), dma((n_pair,)),
        ],
        compiler_params=pltpu.CompilerParams(
            collective_id=0, has_side_effects=True, vmem_limit_bytes=56 * 2**20
        ),
    )(*ids, *args, *large)


def product_kernel(scale, pieces, rows, cols, out, turned, held, sem):
    turned[...] = rows[...].T
    step = out.shape[0] // pieces
    copies = []
    for n in range(pieces):
        at = pl.ds(n * step, step)
        held[at, :] = jnp.dot(turned[at, :], cols[...], preferred_element_type=F32) * scale
        copies.append(pltpu.make_async_copy(held.at[at], out.at[at], sem.at[n]))
        copies[-1].start()
    for copy in copies:
        copy.wait()


def product(rows, cols, n_rows, n_cols, scale):
    depth, row_pad = rows.shape
    pieces = max(x for x in range(1, 9) if n_rows % (16 * x) == 0)
    return pl.pallas_call(
        functools.partial(product_kernel, scale, pieces),
        out_shape=jax.ShapeDtypeStruct((n_rows, n_cols), F32),
        in_specs=[pl.BlockSpec(memory_space=pltpu.VMEM)] * 2,
        out_specs=pl.BlockSpec(memory_space=pl.ANY),
        scratch_shapes=[
            pltpu.VMEM((row_pad, depth), BF16),
            pltpu.VMEM((n_rows, n_cols), F32),
            pltpu.SemaphoreType.DMA((pieces,)),
        ],
        compiler_params=pltpu.CompilerParams(vmem_limit_bytes=48 * 2**20),
    )(rows, cols)


def local(
    valence,
    conduction,
    valence_energy,
    conduction_energy,
    pair_valence,
    pair_conduction,
    pair_count,
    g_index,
):
    slot_count = pair_valence.shape[0]
    total_g = g_index.shape[0]
    n_pair = lax.axis_size("pair")
    n_grow = lax.axis_size("grow")
    n_gcol = lax.axis_size("gcol")
    sub_rows = total_g // (n_pair * n_grow)
    col_width = total_g // n_gcol
    row_pad, col_pad = pad_to(sub_rows, LANES), pad_to(col_width, LANES)
    if row_pad == sub_rows and col_pad == col_width:
        g_list = g_index[None, :]
        col_at = lambda gcol: gcol * col_width
        row_at = lambda pair, grow: (pair * n_grow + grow) * sub_rows
    else:
        by_col = jnp.pad(g_index.reshape(n_gcol, col_width), ((0, 0), (0, col_pad - col_width)))
        by_row = jnp.pad(g_index.reshape(-1, sub_rows), ((0, 0), (0, row_pad - sub_rows)))
        g_list = jnp.concatenate([by_col.reshape(-1), by_row.reshape(-1)])[None, :]
        col_at = lambda gcol: gcol * col_pad
        row_at = lambda pair, grow: n_gcol * col_pad + (pair * n_grow + grow) * row_pad
    chunks = slot_count * n_grow * n_gcol // CHUNK
    layout = (n_pair, n_grow, n_gcol, slot_count, chunks, col_at, row_at)
    cols, rows = panels(
        (pair_valence, pair_conduction, pair_count), valence_energy[None, :], conduction_energy[None, :], g_list,
        valence, conduction, total_g, col_pad, row_pad, layout,
    )
    total_slots = slot_count * n_pair * n_grow * n_gcol
    return product(
        rows.reshape(-1, row_pad), cols.reshape(-1, col_pad), sub_rows, col_width,
        -1.0 / math.sqrt(total_slots),
    )


def solution(mesh):
    return jax.shard_map(
        local,
        mesh=mesh,
        in_specs=(
            P(),
            P("pair", None),
            P(),
            P("pair"),
            P(("pair", "grow", "gcol")),
            P(("pair", "grow", "gcol")),
            P(("pair", "grow", "gcol")),
            P(),
        ),
        out_specs=P(("pair", "grow"), "gcol"),
        check_vma=False,
    )
```

```python
import functools
import math

import jax
import jax.numpy as jnp
import ml_dtypes
import numpy as np
from jax import lax
from jax.experimental import pallas as pl
from jax.experimental.pallas import tpu as pltpu
from jax.sharding import PartitionSpec as P

GRID = 32
BITS = 5
CHUNK = 16
LANES = 128
TILE = 256
MAIN = 256
PIECE = 1152
MESH = pl.DeviceIdType.MESH
BF16 = jnp.bfloat16
F32 = jnp.float32


def pad_to(size, unit):
    return -(-size // unit) * unit


def ball(total_g):
    freq = np.arange(-(GRID // 2) + 1, GRID // 2)
    square = freq[:, None, None] ** 2 + freq[None, :, None] ** 2 + freq[None, None, :] ** 2
    return int(np.sort(square.ravel())[total_g])


def split(values):
    high = values.astype(ml_dtypes.bfloat16)
    low = (values - high.astype(np.float64)).astype(ml_dtypes.bfloat16)
    return high, low


def tables(total_g):
    limit = ball(total_g)
    reach = math.isqrt(limit)
    plane = []
    for b in range(0, reach + 1):
        for c in range(-reach, reach + 1):
            if b * b + c * c <= limit and (b > 0 or c >= 0):
                plane.append((b * b + c * c, b, c))
    plane.sort()
    extra = plane[MAIN:]
    short = math.isqrt(limit - extra[0][0]) if extra else -1
    width = pad_to(len(plane), LANES)
    keys = np.full((width,), -1, np.int32)
    bs = np.zeros((width,), np.int64)
    cs = np.zeros((width,), np.int64)
    for at, (_, b, c) in enumerate(plane):
        keys[at] = b * GRID + c + GRID // 2
        bs[at], cs[at] = b, c
    cell = np.arange(GRID * GRID)
    phase = (cell[:, None] // GRID * bs[None] + cell[:, None] % GRID * cs[None]) % GRID
    angle = phase * (2.0 * math.pi / GRID)
    used = keys[None] >= 0
    first = np.concatenate([np.cos(angle) * used, -np.sin(angle) * used], axis=1)
    points = np.arange(1, GRID // 2 + 1)
    angle = (np.arange(reach + 1)[:, None] * points[None] % GRID) * (2.0 * math.pi / GRID)
    second = np.stack([np.cos(angle), np.sin(angle)])
    second = np.kron(second, np.eye(CHUNK)[None])
    keys = np.repeat(keys[: pad_to(len(plane), CHUNK), None], TILE, axis=1)
    return reach, short, width, keys, split(first), split(second)


def body(
    reach, short, width, layout,
    ids_v, ids_c, count, energy_v_in, energy_c_in, g_list_in, keys_in, valence_in, conduction_in, *refs,
):
    n_pair, n_grow, n_gcol, per_device, chunks, col_at, row_at = layout
    tables_in, (cols, rows), scratch = refs[:4], refs[4:6], refs[6:]
    bands, first_h, first_l, second_h, second_l = scratch[:5]
    infos, dens_h, dens_l, even_h, even_l, odd_h, odd_l, spec, row_buf = scratch[5:14]
    tile_info = infos.at[n_grow * n_gcol]
    load_sem, info_send, info_recv, col_send, col_recv, relay_send, relay_recv, row_send, row_recv = scratch[14:23]
    energy_v, energy_c, g_list, keys = scratch[23:]
    n_v, n_c = valence_in.shape[0], conduction_in.shape[0]

    me, grow, gcol = lax.axis_index("pair"), lax.axis_index("grow"), lax.axis_index("gcol")
    chip, core = me // 2, me % 2
    n_chip, n_group = n_pair // 2, n_grow * n_gcol
    group = grow * n_gcol + gcol
    sibling = {"pair": chip * 2 + (1 - core)}

    def group_id(step):
        other = (group + step) % n_group
        return {"grow": other // n_gcol, "gcol": other % n_gcol}

    def pair_at(step):
        return (chip + 1 + step // 2) % n_chip * 2 + (core + step % 2) % 2

    own_step = (n_chip - 1) * 2

    loads = [
        pltpu.make_async_copy(source, target, load_sem.at[n])
        for n, (source, target) in enumerate(
            zip(
                (valence_in, conduction_in, *tables_in, energy_v_in, energy_c_in, g_list_in, keys_in),
                (bands.at[pl.ds(0, n_v)], bands.at[pl.ds(n_v, n_c)], *scratch[1:5], *scratch[23:]),
            )
        )
    ]
    for load in loads:
        load.start()

    slot = lax.broadcasted_iota(jnp.int32, (CHUNK, LANES), 0) % per_device
    lane = lax.broadcasted_iota(jnp.int32, (CHUNK, LANES), 1)
    mine = jnp.zeros((CHUNK, LANES), jnp.int32)
    for j in range(per_device):
        live = jnp.where(count[0] > j, 1, 0)
        row = jnp.where(lane == 0, ids_v[j], jnp.where(lane == 1, ids_c[j], live))
        mine = jnp.where(slot == j, row, mine)
    tile_info[...] = mine

    barrier = pltpu.get_barrier_semaphore()

    def greet_group(step, carry):
        pl.semaphore_signal(barrier, inc=1, device_id=group_id(step), device_id_type=MESH)
        return carry

    def greet_pair(step, carry):
        @pl.when(step != own_step)
        def _():
            pl.semaphore_signal(
                barrier, inc=1, device_id={"pair": pair_at(step)}, device_id_type=MESH
            )
        return carry

    lax.fori_loop(1, n_group, greet_group, 0)
    lax.fori_loop(0, n_pair, greet_pair, 0)
    pl.semaphore_wait(barrier, n_group - 1 + n_pair - 1)

    def info_copy(step):
        return pltpu.make_async_remote_copy(
            src_ref=tile_info, dst_ref=infos.at[group],
            send_sem=info_send.at[step], recv_sem=info_recv.at[step],
            device_id=group_id(step), device_id_type=MESH,
        )

    def start_info(step, carry):
        info_copy(step).start()
        return carry

    def wait_info(step, carry):
        info_copy(step).wait()
        return carry

    lax.fori_loop(1, n_group, start_info, 0)
    infos[group] = mine
    lax.fori_loop(1, n_group, wait_info, 0)

    plane = GRID * GRID
    together = CHUNK // per_device
    dot = functools.partial(jnp.dot, preferred_element_type=F32)
    for n in (0, 1, 6, 7, 8, 9):
        loads[n].wait()

    def transform(n, first_chunk):
        slot = lax.broadcasted_iota(jnp.int32, (CHUNK, LANES), 0)
        info = jnp.zeros((CHUNK, LANES), jnp.int32)
        for d in range(together):
            info = jnp.where(slot // per_device == d, infos[n * together + d], info)
        pick_v = info[:, 0:1] == lax.broadcasted_iota(jnp.int32, (CHUNK, n_v), 1)
        pick_c = info[:, 1:2] == lax.broadcasted_iota(jnp.int32, (CHUNK, n_c), 1)
        live = info[:, 2:3].astype(F32)
        gap = jnp.sum(jnp.where(pick_c, energy_c[...], 0.0), axis=1, keepdims=True) - jnp.sum(
            jnp.where(pick_v, energy_v[...], 0.0), axis=1, keepdims=True
        )
        factor = live * jnp.sqrt(4.0 / gap) / math.sqrt(GRID**3)
        band = lax.broadcasted_iota(jnp.int32, (CHUNK, n_v + n_c), 1)
        hot = jnp.concatenate(
            [jnp.where(info[:, 0:1] == band, 1.0, 0.0), jnp.where(info[:, 1:2] + n_v == band, 1.0, 0.0)],
            axis=0,
        ).astype(BF16)
        for i in range(GRID):
            at = slice(i * plane, (i + 1) * plane)
            both = dot(hot, bands[:, at])
            dens = both[:CHUNK] * both[CHUNK:]
            high = dens.astype(BF16)
            span = slice(i * CHUNK, (i + 1) * CHUNK)
            dens_h[span, :] = high
            dens_l[span, :] = (dens - high.astype(F32)).astype(BF16)
        if first_chunk:
            loads[2].wait()
            loads[3].wait()
        middle = GRID // 2
        start = []
        for part in range(2):
            at = slice(part * width, (part + 1) * width)
            value = (
                dot(dens_h[...], first_h[:, at])
                + dot(dens_l[...], first_h[:, at])
                + dot(dens_h[...], first_l[:, at])
            ).reshape(GRID, CHUNK, width)
            start.append(value[0])
            for i in range(1, middle + 1):
                span = slice((i - 1) * CHUNK, i * CHUNK)
                even, odd = value[i], jnp.zeros((CHUNK, width), F32)
                if i < middle:
                    even, odd = value[i] + value[GRID - i], value[i] - value[GRID - i]
                for whole, top, rest in ((even, even_h, even_l), (odd, odd_h, odd_l)):
                    high = whole.astype(BF16)
                    top[span, at] = high
                    rest[span, at] = (whole - high.astype(F32)).astype(BF16)
        if first_chunk:
            loads[4].wait()
            loads[5].wait()
        both = []
        for which, top, rest in ((0, even_h, even_l), (1, odd_h, odd_l)):
            value = (
                dot(second_h[which], top[...])
                + dot(second_h[which], rest[...])
                + dot(second_l[which], top[...])
            )
            both.append(value.reshape(reach + 1, CHUNK, 2 * width))
        even, odd = both
        for a in range(reach + 1):
            even_r, even_i = even[a, :, :width] + start[0], even[a, :, width:] + start[1]
            odd_r, odd_i = odd[a, :, :width], odd[a, :, width:]
            parts = [(reach + a, even_r + odd_i, even_i - odd_r)]
            if a:
                parts.append((reach - a, even_r - odd_i, even_i + odd_r))
            for at, real, imag in parts:
                at = 2 * CHUNK * at
                spec[n, at:at + CHUNK, :] = (real * factor).astype(BF16)
                spec[n, at + CHUNK:at + 2 * CHUNK, :] = (imag * factor).astype(BF16)

    transform(0, True)
    if chunks > 1:
        @pl.loop(1, chunks)
        def _(n):
            transform(n, False)

    height = 2 * CHUNK
    low, high = (reach - short) * height, (reach + short + 1) * height

    def select(n, source, size, out, target):
        cell = g_list[:, pl.ds(pl.multiple_of(source, LANES), size)]
        centre = lambda v: jnp.where(v < GRID // 2, v, v - GRID)
        a = centre(cell >> (2 * BITS))
        b = centre((cell >> BITS) & (GRID - 1))
        c = centre(cell & (GRID - 1))
        flip = (b < 0) | ((b == 0) & (c < 0))
        a = jnp.where(flip, -a, a)
        b = jnp.where(flip, -b, b)
        c = jnp.where(flip, -c, c)
        key = b * GRID + c + GRID // 2
        hot = jnp.where(keys[:, :size] == key, 1.0, 0.0).astype(BF16)
        picked = dot(spec[n, :, :MAIN], hot[:MAIN])
        if width > MAIN:
            more = dot(spec[n, low:high, MAIN:keys.shape[0]], hot[MAIN:])
        total = jnp.zeros((height, size), F32)
        for k in range(2 * reach + 1):
            value = picked[k * height:(k + 1) * height]
            if width > MAIN and low <= k * height < high:
                value = value + more[k * height - low:(k + 1) * height - low]
            total = jnp.where(a == k - reach, value, total)
        imag = total[CHUNK:]
        at = pl.ds(target, size)
        out[n, :CHUNK, at] = total[:CHUNK].astype(BF16)
        out[n, CHUNK:, at] = jnp.where(flip, -imag, imag).astype(BF16)

    def block(source, size, out):
        piece = max(x for x in range(LANES, PIECE + 1, LANES) if size % x == 0)

        def run(n):
            def part(t):
                for done in range(0, piece, TILE):
                    at = t * piece + done
                    at = at if isinstance(at, int) else pl.multiple_of(at, LANES)
                    select(n, source + at, min(TILE, piece - done), out, at)

            if size == piece:
                part(0)
            else:
                pl.loop(0, size // piece)(part)

        if chunks == 1:
            run(0)
        else:
            pl.loop(0, chunks)(run)

    def col_copy(step):
        peer = (chip + step) % n_chip * 2 + core
        return pltpu.make_async_remote_copy(
            src_ref=cols.at[me], dst_ref=cols.at[me],
            send_sem=col_send.at[step], recv_sem=col_recv.at[step],
            device_id=sibling if step == 0 else {"pair": peer}, device_id_type=MESH,
        )

    def relay_copy(step):
        source = (chip + n_chip - step) % n_chip * 2 + core
        return pltpu.make_async_remote_copy(
            src_ref=cols.at[source], dst_ref=cols.at[source],
            send_sem=relay_send.at[step], recv_sem=relay_recv.at[step],
            device_id=sibling, device_id_type=MESH,
        )

    def row_copy(step):
        return pltpu.make_async_remote_copy(
            src_ref=row_buf.at[step], dst_ref=rows.at[me],
            send_sem=row_send.at[step], recv_sem=row_recv.at[step],
            device_id={"pair": pair_at(step)}, device_id_type=MESH,
        )

    block(col_at(gcol), cols.shape[-1], cols.at[me])
    for step in (*range(1, n_chip), 0):
        col_copy(step).start()

    def row_step(step, carry):
        block(row_at(pair_at(step), grow), rows.shape[-1], row_buf.at[step])

        @pl.when(step != own_step)
        def _():
            row_copy(step).start()
        return carry

    lax.fori_loop(0, own_step, row_step, 0)
    for step in range(1, n_chip):
        col_copy(step).wait_recv()
        relay_copy(step).start()
    lax.fori_loop(own_step, n_pair, row_step, 0)
    rows[me] = row_buf[own_step]

    for step in range(1, n_chip):
        col_copy(step).wait_send()
        relay_copy(step).wait()
    col_copy(0).wait()

    def row_wait(step, carry):
        @pl.when(step != own_step)
        def _():
            row_copy(step).wait()
        return carry

    lax.fori_loop(0, n_pair, row_wait, 0)


def panels(ids, energy_v, energy_c, g_list, valence, conduction, total_g, col_pad, row_pad, layout):
    reach, short, width, keys, first, second = tables(total_g)
    n_pair, n_grow, n_gcol, per_device, chunks = layout[:5]
    consts = [jnp.asarray(x) for x in (*first, *second)]
    large = [valence, conduction, *consts]
    args = [energy_v, energy_c, g_list, jnp.asarray(keys)]
    height = 2 * CHUNK * (2 * reach + 1)
    half = GRID * CHUNK
    n_group = n_grow * n_gcol
    n_v, n_c = valence.shape[0], conduction.shape[0]
    vmem = pl.BlockSpec(memory_space=pltpu.VMEM)
    dma = pltpu.SemaphoreType.DMA
    return pl.pallas_call(
        functools.partial(body, reach, short, width, layout),
        out_shape=[
            pltpu.VMEM((n_pair, chunks, 2 * CHUNK, col_pad), BF16),
            pltpu.VMEM((n_pair, chunks, 2 * CHUNK, row_pad), BF16),
        ],
        in_specs=[pl.BlockSpec(memory_space=pltpu.SMEM)] * len(ids) + [pl.BlockSpec(memory_space=pl.ANY)] * len(args)
        + [pl.BlockSpec(memory_space=pl.ANY)] * len(large),
        out_specs=[vmem] * 2,
        scratch_shapes=[pltpu.VMEM((n_v + n_c, GRID**3), BF16)]
        + [pltpu.VMEM(x.shape, x.dtype) for x in consts] + [
            pltpu.VMEM((n_group + 1, CHUNK, LANES), jnp.int32),
            pltpu.VMEM((half, GRID * GRID), BF16),
            pltpu.VMEM((half, GRID * GRID), BF16),
            *[pltpu.VMEM((half // 2, 2 * width), BF16)] * 4,
            pltpu.VMEM((chunks, height, width), BF16),
            pltpu.VMEM((n_pair, chunks, 2 * CHUNK, row_pad), BF16),
            dma((len(large) + len(args),)),
            dma((n_group,)), dma((n_group,)),
            dma((n_pair // 2,)), dma((n_pair // 2,)),
            dma((n_pair // 2,)), dma((n_pair // 2,)),
            dma((n_pair,)), dma((n_pair,)),
            *[pltpu.VMEM(x.shape, x.dtype) for x in args],
        ],
        compiler_params=pltpu.CompilerParams(
            collective_id=0, has_side_effects=True, vmem_limit_bytes=56 * 2**20
        ),
    )(*ids, *args, *large)


def product_kernel(scale, pieces, rows, cols, out, turned, held, sem):
    turned[...] = rows[...].T
    step = out.shape[0] // pieces
    copies = []
    for n in range(pieces):
        at = pl.ds(n * step, step)
        held[at, :] = jnp.dot(turned[at, :], cols[...], preferred_element_type=F32) * scale
        copies.append(pltpu.make_async_copy(held.at[at], out.at[at], sem.at[n]))
        copies[-1].start()
    for copy in copies:
        copy.wait()


def product(rows, cols, n_rows, n_cols, scale):
    depth, row_pad = rows.shape
    pieces = max(x for x in range(1, 9) if n_rows % (16 * x) == 0)
    return pl.pallas_call(
        functools.partial(product_kernel, scale, pieces),
        out_shape=jax.ShapeDtypeStruct((n_rows, n_cols), F32),
        in_specs=[pl.BlockSpec(memory_space=pltpu.VMEM)] * 2,
        out_specs=pl.BlockSpec(memory_space=pl.ANY),
        scratch_shapes=[
            pltpu.VMEM((row_pad, depth), BF16),
            pltpu.VMEM((n_rows, n_cols), F32),
            pltpu.SemaphoreType.DMA((pieces,)),
        ],
        compiler_params=pltpu.CompilerParams(vmem_limit_bytes=48 * 2**20),
    )(rows, cols)


def local(
    valence,
    conduction,
    valence_energy,
    conduction_energy,
    pair_valence,
    pair_conduction,
    pair_count,
    g_index,
):
    slot_count = pair_valence.shape[0]
    total_g = g_index.shape[0]
    n_pair = lax.axis_size("pair")
    n_grow = lax.axis_size("grow")
    n_gcol = lax.axis_size("gcol")
    sub_rows = total_g // (n_pair * n_grow)
    col_width = total_g // n_gcol
    row_pad, col_pad = pad_to(sub_rows, LANES), pad_to(col_width, LANES)
    if row_pad == sub_rows and col_pad == col_width:
        g_list = g_index[None, :]
        col_at = lambda gcol: gcol * col_width
        row_at = lambda pair, grow: (pair * n_grow + grow) * sub_rows
    else:
        by_col = jnp.pad(g_index.reshape(n_gcol, col_width), ((0, 0), (0, col_pad - col_width)))
        by_row = jnp.pad(g_index.reshape(-1, sub_rows), ((0, 0), (0, row_pad - sub_rows)))
        g_list = jnp.concatenate([by_col.reshape(-1), by_row.reshape(-1)])[None, :]
        col_at = lambda gcol: gcol * col_pad
        row_at = lambda pair, grow: n_gcol * col_pad + (pair * n_grow + grow) * row_pad
    chunks = slot_count * n_grow * n_gcol // CHUNK
    layout = (n_pair, n_grow, n_gcol, slot_count, chunks, col_at, row_at)
    cols, rows = panels(
        (pair_valence, pair_conduction, pair_count), valence_energy[None, :], conduction_energy[None, :], g_list,
        valence, conduction, total_g, col_pad, row_pad, layout,
    )
    total_slots = slot_count * n_pair * n_grow * n_gcol
    return product(
        rows.reshape(-1, row_pad), cols.reshape(-1, col_pad), sub_rows, col_width,
        -1.0 / math.sqrt(total_slots),
    )


def solution(mesh):
    return jax.shard_map(
        local,
        mesh=mesh,
        in_specs=(
            P(),
            P("pair", None),
            P(),
            P("pair"),
            P(("pair", "grow", "gcol")),
            P(("pair", "grow", "gcol")),
            P(("pair", "grow", "gcol")),
            P(),
        ),
        out_specs=P(("pair", "grow"), "gcol"),
        check_vma=False,
    )
```
